32 devices in a mesh: seq: 8 (over z, y), wt: 4 (over x, core).
Axes of the slice: x: 2, y: 2, z: 4, core: 2. Of those that a mesh axis runs over, the one named last changes fastest.
Arguments:
- inputs: bfloat16 [8, 512, 2560], P('wt', 'seq'), may hold values from -6 to 6
- positions: int32 [8, 512], P('wt', 'seq'), may hold values from 0 to 479, as said below
- cotangent: bfloat16 [8, 512, 2560], P('wt', 'seq'), may hold values from -6 to 6
- gain: float32 [2560], replicated, may hold values from 0.1 to 1.9
- w_x: bfloat16 [2560, 2560], P('wt'), may hold values from -0.125 to 0.125
- w_y: bfloat16 [2560, 2560], P('wt'), may hold values from -0.125 to 0.125
- conv_w: float32 [4, 2560], replicated, may hold values from -3 to 3
- conv_b: float32 [2560], replicated, may hold values from -3 to 3
- gate_a: bfloat16 [2560, 256], P('wt'), may hold values from -0.375 to 0.375
- bias_a: float32 [2560], replicated, may hold values from -4 to 4
- gate_i: bfloat16 [2560, 256], P('wt'), may hold values from -0.375 to 0.375
- bias_i: float32 [2560], replicated, may hold values from -3 to 3
- decay_log: float32 [2560], replicated
- w_out: bfloat16 [2560, 2560], P('wt'), may hold values from -0.125 to 0.125
- gain2: float32 [2560], replicated, may hold values from 0.1 to 1.9
- w_gate: bfloat16 [2560, 7680], P(None, 'wt'), may hold values from -0.125 to 0.125
- w_up: bfloat16 [2560, 7680], P(None, 'wt'), may hold values from -0.125 to 0.125
- w_down: bfloat16 [7680, 2560], P('wt'), may hold values from -0.0625 to 0.0625
Outputs:
- result: bfloat16 [8, 512, 2560], P('wt', 'seq')
- input_grad: float32 [8, 512, 2560], P('wt', 'seq')
- grad_gain: float32 [2560], P(('seq', 'wt'))
- grad_w_x: float32 [2560, 2560], P(('seq', 'wt'))
- grad_w_y: float32 [2560, 2560], P(('seq', 'wt'))
- grad_conv_w: float32 [4, 2560], P(None, ('seq', 'wt'))
- grad_conv_b: float32 [2560], P(('seq', 'wt'))
- grad_gate_a: float32 [2560, 256], P(('seq', 'wt'))
- grad_bias_a: float32 [2560], P(('seq', 'wt'))
- grad_gate_i: float32 [2560, 256], P(('seq', 'wt'))
- grad_bias_i: float32 [2560], P(('seq', 'wt'))
- grad_decay: float32 [2560], P(('seq', 'wt'))
- grad_w_out: float32 [2560, 2560], P(('seq', 'wt'))
- grad_gain2: float32 [2560], P(('seq', 'wt'))
- grad_w_gate: float32 [2560, 7680], P('seq', 'wt')
- grad_w_up: float32 [2560, 7680], P('seq', 'wt')
- grad_w_down: float32 [7680, 2560], P('wt', 'seq')
The draws below stay inside these ranges and needn't reach their ends.
Inputs may be any that keep to these rules, and one draw needn't show every extreme that they name: `positions`: 0 at a document's first token and one more than the token before otherwise; every sequence starts a document at its first token; in every sequence one document of exactly 480 tokens starts within its first 64 tokens and runs into its last 64 tokens.
All inputs are finite; a program needn't handle non-finite values.
Results may differ from the reference program's by a relative error of at most 0.018.
Values may be sent and summed in bfloat16 or wider, within the bound.
No kernel may reach another device: no remote copies, remote signals or barrier semaphores. Data moves between devices by JAX's collectives and lax.ppermute only.
A program may use at most 640 MiB of HBM per device.

```python
import jax
import jax.numpy as jnp
from jax import lax

D = 2560
HD = 256
FF = 7680
HEADS = 10
CONV = 4
TOK_MB = 64
SEQ_LEN = 512
BATCHES = 8


def draw_positions(key, part):
    key = jax.random.fold_in(key, 5)

    def one_sequence(seq_key):
        subkeys = jax.random.split(seq_key, 2)
        margin = max(TOK_MB // 2, 1)
        opening = jax.random.randint(subkeys[0], (), 0, margin)
        finish = opening + SEQ_LEN - margin
        places = jnp.arange(SEQ_LEN, dtype=jnp.int32)
        scattered = jax.random.randint(subkeys[1], (SEQ_LEN,), 0, 8) == 0
        outside = (places < opening) | (places > finish)
        starts = (places == 0) | (places == opening) | (places == finish) | scattered & outside
        starts_at = jnp.where(starts, places, 0)
        return places - lax.cummax(starts_at, axis=0)
    return jax.vmap(one_sequence)(jax.random.split(key, BATCHES))


def draw_decay_log(key, part):
    key = jax.random.fold_in(key, 9)
    subkeys = jax.random.split(key, 2)
    spread = jax.random.uniform(subkeys[0], (D,), jnp.float32)
    choose = jax.random.uniform(subkeys[1], (D,), jnp.float32)
    slow_share = 0.5
    slow_rate = jnp.log(0.05 / SEQ_LEN) + spread * jnp.log(10.0)
    fast_rate = jnp.log(1.0 / 200.0) + spread * jnp.log(200.0 / 120.0)
    return jnp.where(choose < slow_share, slow_rate, fast_rate).astype(jnp.float32)


def steps_of(own_key, shape, cuts, least, largest):
    level = 1.0
    for position, blocks in cuts:
        steps = jax.random.uniform(jax.random.fold_in(jax.random.fold_in(own_key, 6), position), (blocks,), jnp.float32, least / len(cuts), largest / len(cuts))
        level = level * jnp.repeat(jnp.exp(steps), shape[position] // blocks).reshape((-1,) + (1,) * (len(shape) - 1 - position))
    return level


def centred(stream_key, shape, deviation, most, shards=(), held_as=jnp.bfloat16):
    factor_of = steps_of(stream_key, shape, shards, -0.22, 0.18) if shards else 1.0
    entries = jax.random.normal(stream_key, shape, jnp.float32) * deviation * factor_of
    return jnp.minimum(jnp.maximum(entries, -most), most).astype(held_as)


def setup_inputs(seed: int = 0) -> dict:
    splits = jax.random.split(jax.random.key(seed), 19)
    inputs = centred(splits[0], (BATCHES, SEQ_LEN, D), 1.0, 6.0, ((0, 4), (1, 8)))
    positions = draw_positions(jax.random.fold_in(splits[18], 71), 0)
    cotangent = centred(splits[2], (BATCHES, SEQ_LEN, D), 1.0, 6.0, ((0, 4), (1, 8)))
    gain = jnp.clip(1.0 + 0.18 * jax.random.normal(splits[3], (D,), jnp.float32), 0.1, 1.9)
    w_x = centred(splits[4], (D, D), D ** -0.5, 0.125, ((0, 4),))
    w_y = centred(splits[5], (D, D), D ** -0.5, 0.125, ((0, 4),))
    conv_w = centred(splits[6], (CONV, D), 0.5, 3.0, (), jnp.float32)
    conv_b = centred(splits[7], (D,), 0.5, 3.0, (), jnp.float32)
    gate_a = centred(splits[8], (D, HD), HD ** -0.5, 0.375, ((0, 4),))
    bias_a = centred(splits[9], (D,), 1.0, 4.0, (), jnp.float32)
    gate_i = centred(splits[10], (D, HD), HD ** -0.5, 0.375, ((0, 4),))
    bias_i = centred(splits[11], (D,), 0.5, 3.0, (), jnp.float32)
    decay_log = draw_decay_log(jax.random.fold_in(splits[18], 71), 0)
    w_out = centred(splits[13], (D, D), D ** -0.5, 0.125, ((0, 4),))
    gain2 = jnp.clip(1.0 + 0.18 * jax.random.normal(splits[14], (D,), jnp.float32), 0.1, 1.9)
    w_gate = centred(splits[15], (D, FF), D ** -0.5, 0.125, ((1, 4),))
    w_up = centred(splits[16], (D, FF), D ** -0.5, 0.125, ((1, 4),))
    w_down = centred(splits[17], (FF, D), FF ** -0.5, 0.0625, ((0, 4),))
    return {"inputs": inputs, "positions": positions, "cotangent": cotangent, "gain": gain, "w_x": w_x, "w_y": w_y, "conv_w": conv_w, "conv_b": conv_b, "gate_a": gate_a, "bias_a": bias_a, "gate_i": gate_i, "bias_i": bias_i, "decay_log": decay_log, "w_out": w_out, "gain2": gain2, "w_gate": w_gate, "w_up": w_up, "w_down": w_down}


@jax.custom_vjp
def low(v):
    return lax.optimization_barrier(v.astype(jnp.bfloat16)).astype(jnp.float32)

@jax.custom_vjp
def low_back(v):
    return v

def low_keep(v):
    return (low(v), None)

def low_pass(kept, grad):
    return (grad,)

def back_keep(v):
    return (v, None)

def back_low(kept, grad):
    return (low(grad),)
low.defvjp(low_keep, low_pass)
low_back.defvjp(back_keep, back_low)

def highest(left, right):
    return jnp.dot(left, right, precision=lax.Precision.HIGHEST)

def combine(earlier, latter):
    return (latter[0] * earlier[0], latter[1] + latter[0] * earlier[1])

def blockwise(values, weight):
    length = values.shape[0]
    shaped = values.reshape(length, HEADS, HD)
    blocks = weight.reshape(HEADS, HD, HD)
    return jnp.einsum('thi,hij->thj', shaped, blocks, precision=lax.Precision.HIGHEST).reshape(length, D)

def one_sequence(weights_all, sequence, doc_place):
    gain, w_x, w_y, conv_w, conv_b, gate_a, bias_a, gate_i, bias_i, decay_log, w_out, gain2, w_gate, w_up, w_down = weights_all
    length = sequence.shape[0]
    norm_scale = lax.rsqrt(lax.optimization_barrier(jnp.mean(sequence * sequence, axis=-1, keepdims=True)) + 1e-06)
    normed = low(sequence * norm_scale * gain)
    branch_x = low_back(low(highest(normed, w_x)))
    branch_pre = low_back(highest(normed, w_y))
    branch_y = jax.nn.gelu(branch_pre, approximate=True)
    padded = jnp.concatenate([jnp.zeros((CONV - 1, D), jnp.float32), branch_x], axis=0)
    total = conv_b + jnp.zeros((length, D), jnp.float32)
    for offset in range(CONV):
        shifted = padded[CONV - 1 - offset:CONV - 1 - offset + length]
        total = total + conv_w[offset] * shifted * (doc_place >= offset).astype(jnp.float32)[:, None]
    conv_out = low_back(low(total))
    logit_a = low_back(blockwise(conv_out, gate_a))
    logit_i = low_back(blockwise(conv_out, gate_i))
    gate_rec = jax.nn.sigmoid(logit_a + bias_a)
    gate_in = jax.nn.sigmoid(logit_i + bias_i)
    log_a = -8.0 * gate_rec * jnp.exp(decay_log)
    alive_mask = (doc_place > 0).astype(jnp.float32)[:, None]
    root_term = jnp.sqrt(-jnp.expm1(2.0 * log_a))
    multiplier = alive_mask * root_term + (1.0 - alive_mask)
    decay = jnp.exp(log_a) * alive_mask
    driven = conv_out * gate_in * multiplier
    unused_product, state_all = lax.associative_scan(combine, (decay, driven), axis=0)
    mixed_rows = low(state_all * branch_y)
    projected = low_back(highest(mixed_rows, w_out))
    stream = sequence + projected
    second_scale = lax.rsqrt(lax.optimization_barrier(jnp.mean(stream * stream, axis=-1, keepdims=True)) + 1e-06)
    normed_two = low(stream * second_scale * gain2)
    gate_pre = low_back(highest(normed_two, w_gate))
    up_pre = low_back(highest(normed_two, w_up))
    hidden = low(jax.nn.gelu(gate_pre, approximate=True) * up_pre)
    return stream + highest(hidden, w_down)

def reference(inputs, positions, cotangent, gain, w_x, w_y, conv_w, conv_b, gate_a, bias_a, gate_i, bias_i, decay_log, w_out, gain2, w_gate, w_up, w_down):
    weights_all = tuple((weight.astype(jnp.float32) for weight in (gain, w_x, w_y, conv_w, conv_b, gate_a, bias_a, gate_i, bias_i, decay_log, w_out, gain2, w_gate, w_up, w_down)))
    source = inputs.astype(jnp.float32)

    def forward(weights_all, source):

        def per_sequence(sample):
            return one_sequence(weights_all, sample[0], sample[1])
        return lax.map(jax.checkpoint(per_sequence), (source, positions))
    output, pull_back = jax.vjp(forward, weights_all, source)
    grads, input_grad = pull_back(cotangent.astype(jnp.float32))
    return (output.astype(jnp.bfloat16), input_grad, grads[0], grads[1], grads[2], grads[3], grads[4], grads[5], grads[6], grads[7], grads[8], grads[9], grads[10], grads[11], grads[12], grads[13], grads[14])
```

```python
from functools import partial

import jax
import jax.numpy as jnp
from jax import lax
from jax.experimental import pallas as pl
from jax.experimental.pallas import tpu as pltpu
from jax.sharding import Mesh
from jax.sharding import PartitionSpec as P

SZ, SY, WX, WC = ("sz", "sy", "wx", "wc")
F32, BF16 = (jnp.float32, jnp.bfloat16)
HALO = 8
ROOT_2_PI = 0.7978845608028654
CUBIC = 0.044715
MIB = 1 << 20


def swap(value, axis):
    return lax.ppermute(value, axis, [(0, 1), (1, 0)])


def shift(value, axis, steps):
    count = lax.axis_size(axis)
    initial, last = (max(0, -steps), min(count, count - steps))
    return lax.ppermute(value, axis, [(source, source + steps) for source in range(initial, last)])


def along_seq(value, steps):
    count = lax.axis_size(SZ) * lax.axis_size(SY)
    initial, last = (max(0, -steps), min(count, count - steps))
    return lax.ppermute(
        value, (SZ, SY), [(source, source + steps) for source in range(initial, last)]
    )


def pick(bit, zero, one):
    return jnp.where(bit == 0, zero, one)


def after(value, *others):
    return lax.optimization_barrier((value, *others))[0]


def gelu_pair(value):
    square = value * value
    tanh = jnp.tanh(ROOT_2_PI * value * (1.0 + CUBIC * square))
    half = 0.5 * (1.0 + tanh)
    slope = half + 0.5 * value * (1.0 - tanh * tanh) * (
        ROOT_2_PI * (1.0 + 3.0 * CUBIC * square)
    )
    return value * half, slope


def dot(left, right):
    return jnp.dot(left, right, preferred_element_type=F32)


def dot_nt(left, right):
    return lax.dot_general(left, right, (((1,), (1,)), ((), ())), preferred_element_type=F32)


def dot_tn(left, right):
    return lax.dot_general(left, right, (((0,), (0,)), ((), ())), preferred_element_type=F32)


def params(mib):
    return pltpu.CompilerParams(
        dimension_semantics=("arbitrary",), vmem_limit_bytes=mib * MIB
    )


def cost(flops, nbytes):
    return pl.CostEstimate(flops=int(flops), bytes_accessed=int(nbytes), transcendentals=0)


def split_columns(value, wx, wc):
    quarter = value.shape[-1] // 4
    parts = [value[..., i * quarter : (i + 1) * quarter] for i in range(4)]
    near = [pick(wx, parts[0], parts[2]), pick(wx, parts[1], parts[3])]
    far = [pick(wx, parts[2], parts[0]), pick(wx, parts[3], parts[1])]
    keep = jnp.concatenate([pick(wc, near[0], near[1]), pick(wc, near[1], near[0])], axis=-1)
    send = jnp.concatenate([pick(wc, far[0], far[1]), pick(wc, far[1], far[0])], axis=-1)
    return keep, send


def join_columns(near, far, wx, wc):
    near = [pick(wc, near[0], near[1]), pick(wc, near[1], near[0])]
    far = [pick(wc, far[0], far[1]), pick(wc, far[1], far[0])]
    return jnp.concatenate(
        [
            pick(wx, near[0], far[0]),
            pick(wx, near[1], far[1]),
            pick(wx, far[0], near[0]),
            pick(wx, far[1], near[1]),
        ],
        axis=-1,
    )


def project_kernel(recv, keep, w_own, w_oth, send_out, own_out, left):
    rows, quarter = recv.shape[0], w_own.shape[0]

    @pl.when(pl.program_id(0) == 0)
    def _():
        left[:rows] = recv[...]
        left[rows:] = keep[...]

    total = dot(left[:, :quarter], w_own[...]) + dot(left[:, quarter:], w_oth[...])
    send_out[...] = total[:rows].astype(BF16)
    own_out[...] = total[rows:]


def project(recv, keep, w_own, w_oth):
    rows, half = recv.shape
    quarter, width = w_own.shape
    tile = 512
    whole = pl.BlockSpec((rows, half), lambda j: (0, 0))
    column = pl.BlockSpec((quarter, tile), lambda j: (0, j))
    out = pl.BlockSpec((rows, tile), lambda j: (0, j))
    return pl.pallas_call(
        project_kernel,
        grid=(width // tile,),
        in_specs=[whole, whole, column, column],
        out_specs=[out, out],
        out_shape=[
            jax.ShapeDtypeStruct((rows, width), BF16),
            jax.ShapeDtypeStruct((rows, width), F32),
        ],
        scratch_shapes=[pltpu.VMEM((2 * rows, half), BF16)],
        compiler_params=params(32),
        cost_estimate=cost(4 * rows * half * width, 4 * half * width),
        name="project",
    )(recv, keep, w_own, w_oth)


def project_back_kernel(count, *refs):
    tokens, weights = refs[: 2 * count], refs[2 * count : 4 * count]
    send_out, own_out = refs[4 * count : 4 * count + 2]
    lefts = refs[4 * count + 2 :]
    rows = tokens[0].shape[0]

    @pl.when(pl.program_id(0) == 0)
    def _():
        for i in range(count):
            lefts[i][:rows] = tokens[2 * i][...]
            lefts[i][rows:] = tokens[2 * i + 1][...]

    total = None
    for i in range(count):
        right = jnp.concatenate([weights[2 * i][...], weights[2 * i + 1][...]], axis=0)
        term = dot_nt(lefts[i][...], right)
        total = term if total is None else total + term
    tile = total.shape[1] // 2
    for i in range(2):
        send_out[i] = total[:rows, i * tile : (i + 1) * tile].astype(BF16)
        own_out[i] = total[rows:, i * tile : (i + 1) * tile]


def project_back(terms):
    count = len(terms)
    rows, width = terms[0][0].shape
    quarter = terms[0][2].shape[0]
    tile = 128
    whole = pl.BlockSpec((rows, width), lambda j: (0, 0))
    row = pl.BlockSpec((tile, width), lambda j: (j, 0))
    out = pl.BlockSpec((2, rows, tile), lambda j: (0, 0, j))
    return pl.pallas_call(
        partial(project_back_kernel, count),
        grid=(quarter // tile,),
        in_specs=[whole] * (2 * count) + [row] * (2 * count),
        out_specs=[out, out],
        out_shape=[
            jax.ShapeDtypeStruct((2, rows, quarter), BF16),
            jax.ShapeDtypeStruct((2, rows, quarter), F32),
        ],
        scratch_shapes=[pltpu.VMEM((2 * rows, width), BF16)] * count,
        compiler_params=params(40),
        cost_estimate=cost(
            8 * count * rows * quarter * width, 4 * count * quarter * width
        ),
        name="project_back",
    )(*[t for term in terms for t in term[:2]], *[w for term in terms for w in term[2:]])


def less_one_exp(value):
    series = 1.0
    for n in (9, 8, 7, 6, 5, 4, 3, 2):
        series = 1.0 + value * (1.0 / n) * series
    return jnp.where(value > -0.5, -value * series, 1.0 - jnp.exp(value))


def shifted_down(value, steps, fill):
    edge = jnp.full((value.shape[0], steps, value.shape[2]), fill, F32)
    return jnp.concatenate([edge, value[:, : value.shape[1] - steps]], axis=1)


def shifted_up(value, steps, fill):
    edge = jnp.full((value.shape[0], steps, value.shape[2]), fill, F32)
    return jnp.concatenate([value[:, steps:], edge], axis=1)


def scan_rows(decay, driven, mover):
    steps = 1
    while steps < decay.shape[1]:
        driven = driven + decay * mover(driven, steps, 0.0)
        decay = decay * mover(decay, steps, 1.0)
        steps *= 2
    return decay, driven


def tap_mask(places, offset):
    return (places >= offset).astype(F32)


def recur_kernel(
    own,
    recv,
    halo,
    places,
    conv_w,
    conv_b,
    gate_a,
    gate_i,
    bias_a,
    bias_i,
    decay_log,
    branch_out,
    conv_out,
    rec_out,
    in_out,
    run_out,
    state_out,
    ends_out,
):
    batches, length, width = own.shape
    branch = (own[...] + recv[...].astype(F32)).astype(BF16)
    branch_out[...] = branch
    extended = jnp.concatenate([halo[...], branch.astype(F32)], axis=1)
    spot = places[...]
    total = jnp.zeros((batches, length, width), F32) + conv_b[...][None]
    for offset in range(conv_w.shape[0]):
        moved = extended[:, HALO - offset : HALO - offset + length]
        total = total + conv_w[offset : offset + 1][None] * moved * tap_mask(spot, offset)
    conv = total.astype(BF16)
    conv_out[...] = conv
    flat = conv.reshape(batches * length, width)
    shape = (batches, length, width)
    gate_rec = jax.nn.sigmoid(dot(flat, gate_a[...]) + bias_a[...]).reshape(shape)
    gate_in = jax.nn.sigmoid(dot(flat, gate_i[...]) + bias_i[...]).reshape(shape)
    rec_out[...] = gate_rec
    in_out[...] = gate_in
    log_a = -8.0 * gate_rec * jnp.exp(decay_log[...])[None]
    alive = tap_mask(spot, 1)
    root = jnp.sqrt(less_one_exp(2.0 * log_a))
    multiplier = alive * root + (1.0 - alive)
    decay = jnp.exp(log_a) * alive
    driven = conv.astype(F32) * gate_in * multiplier
    running, state = scan_rows(decay, driven, shifted_down)
    run_out[...] = running
    state_out[...] = state
    for b in range(batches):
        ends_out[b : b + 1] = running[b, length - 1 :]
        ends_out[batches + b : batches + b + 1] = state[b, length - 1 :]


def head_specs(batches, length, head, taps):
    tokens = pl.BlockSpec((batches, length, head), lambda h: (0, 0, h))
    edge = pl.BlockSpec((batches, HALO, head), lambda h: (0, 0, h))
    place = pl.BlockSpec((batches, length, 1), lambda h: (0, 0, 0))
    row = pl.BlockSpec((1, head), lambda h: (0, h))
    tap = pl.BlockSpec((taps, head), lambda h: (0, h))
    gates = [
        pl.BlockSpec((head, head), lambda h: (h, 0)),
        pl.BlockSpec((head, head), lambda h: (h, 1)),
    ]
    ends = pl.BlockSpec((2 * batches, head), lambda h: (0, h))
    carry = pl.BlockSpec((batches, 1, head), lambda h: (0, 0, h))
    return tokens, edge, place, row, tap, gates, ends, carry


def recur(own, recv, halo, places, conv_w, conv_b, gates, bias_a, bias_i, decay_log):
    batches, length, features = own.shape
    head = gates.shape[1] // 2
    tokens, edge, place, row, tap, gate, ends, _ = head_specs(
        batches, length, head, conv_w.shape[0]
    )
    full = lambda dtype: jax.ShapeDtypeStruct((batches, length, features), dtype)
    return pl.pallas_call(
        recur_kernel,
        grid=(features // head,),
        in_specs=[tokens, tokens, edge, place, tap, row, *gate, row, row, row],
        out_specs=[tokens] * 6 + [ends],
        out_shape=[full(BF16), full(BF16)]
        + [full(F32)] * 4
        + [jax.ShapeDtypeStruct((2 * batches, features), F32)],
        compiler_params=params(32),
        cost_estimate=cost(200 * batches * length * features, 40 * batches * length * features),
        name="recur",
    )(own, recv, halo, places, conv_w, conv_b, gates, gates, bias_a, bias_i, decay_log)


def unroll_kernel(
    mixed_grad,
    own_y,
    recv_y,
    running,
    local_state,
    carry,
    gate_rec,
    places,
    decay_log,
    pre_out,
    behind_out,
    local_out,
    ends_out,
):
    batches, length, _ = mixed_grad.shape
    pulled = mixed_grad[...].astype(F32)
    branch_y, slope = gelu_pair(own_y[...] + recv_y[...].astype(F32))
    state = local_state[...] + running[...] * carry[...]
    pre_out[...] = (pulled * state * slope).astype(BF16)
    log_a = -8.0 * gate_rec[...] * jnp.exp(decay_log[...])[None]
    decay = jnp.exp(log_a) * tap_mask(places[...], 1)
    following = shifted_up(decay, 1, 1.0)
    behind, local = scan_rows(following, pulled * branch_y, shifted_up)
    behind_out[...] = behind
    local_out[...] = local
    for b in range(batches):
        ends_out[b : b + 1] = running[b, length - 1 :, :]
        ends_out[batches + b : batches + b + 1] = decay[b, :1] * local[b, :1]


def unroll(mixed_grad, own_y, recv_y, running, local_state, carry, gate_rec, places, decay_log, head):
    batches, length, features = mixed_grad.shape
    tokens, _, place, row, _, _, ends, carried = head_specs(batches, length, head, 1)
    full = lambda dtype: jax.ShapeDtypeStruct((batches, length, features), dtype)
    return pl.pallas_call(
        unroll_kernel,
        grid=(features // head,),
        in_specs=[tokens] * 5 + [carried, tokens, place, row],
        out_specs=[tokens] * 3 + [ends],
        out_shape=[full(BF16), full(F32), full(F32)]
        + [jax.ShapeDtypeStruct((2 * batches, features), F32)],
        compiler_params=params(32),
        cost_estimate=cost(200 * batches * length * features, 40 * batches * length * features),
        name="unroll",
    )(mixed_grad, own_y, recv_y, running, local_state, carry, gate_rec, places, decay_log)


def recur_back_kernel(
    behind,
    local_grad,
    carry_back,
    running,
    local_state,
    carry,
    gate_rec,
    gate_in,
    conv,
    branch,
    halo,
    places,
    conv_w,
    gate_a,
    gate_i,
    decay_log,
    spread_out,
    earlier_out,
    wa_out,
    wi_out,
    sums_out,
):
    batches, length, width = behind.shape
    shape = (batches, length, width)
    rows = batches * length
    spot = places[...]
    alive = tap_mask(spot, 1)
    rate = jnp.exp(decay_log[...])[None]
    rec, inner = gate_rec[...], gate_in[...]
    log_a = -8.0 * rec * rate
    raw = jnp.exp(log_a)
    root = jnp.sqrt(less_one_exp(2.0 * log_a))
    multiplier = alive * root + (1.0 - alive)
    conv_low = conv[...]
    conv_full = conv_low.astype(F32)
    grad_state = local_grad[...] + behind[...] * carry_back[...]
    state = local_state[...] + running[...] * carry[...]
    before = jnp.concatenate([carry[...], state[:, : length - 1]], axis=1)
    scaled = grad_state * conv_full * inner
    grad_log = alive * raw * (grad_state * before - scaled * raw / root)
    grad_a = grad_log * (-8.0 * rate) * rec * (1.0 - rec)
    grad_i = scaled * multiplier * (1.0 - inner)
    low_a = grad_a.astype(BF16).reshape(rows, width)
    low_i = grad_i.astype(BF16).reshape(rows, width)
    pulled = grad_state * inner * multiplier
    pulled = pulled + (dot_nt(low_a, gate_a[...]) + dot_nt(low_i, gate_i[...])).reshape(shape)
    pulled = pulled.astype(BF16).astype(F32)
    flat = conv_low.reshape(rows, width)
    wa_out[...] = dot_tn(flat, low_a).astype(BF16)
    wi_out[...] = dot_tn(flat, low_i).astype(BF16)
    extended = jnp.concatenate([halo[...], branch[...].astype(F32)], axis=1)
    taps = conv_w.shape[0]
    spread = jnp.zeros((batches, length + HALO, width), F32)
    blank = jnp.zeros((batches, HALO, width), F32)
    sums = []
    add = lambda value: jnp.sum(value.reshape(rows, width), axis=0, keepdims=True)
    for offset in range(taps):
        masked = pulled * tap_mask(spot, offset)
        weighted = jnp.concatenate([blank, conv_w[offset : offset + 1][None] * masked], axis=1)
        spread = spread + (shifted_up(weighted, offset, 0.0) if offset else weighted)
        sums.append(add(masked * extended[:, HALO - offset : HALO - offset + length]))
    earlier_out[...] = spread[:, :HALO]
    spread_out[...] = spread[:, HALO:]
    sums += [add(pulled), add(grad_a), add(grad_i), add(grad_log * log_a)]
    sums_out[...] = jnp.concatenate(sums, axis=0)


def recur_back(
    behind,
    local_grad,
    carry_back,
    running,
    local_state,
    carry,
    gate_rec,
    gate_in,
    conv,
    branch,
    halo,
    places,
    conv_w,
    gates,
    decay_log,
):
    batches, length, features = behind.shape
    head = gates.shape[1] // 2
    taps = conv_w.shape[0]
    tokens, edge, place, row, tap, gate, _, carried = head_specs(batches, length, head, taps)
    block = pl.BlockSpec((head, head), lambda h: (h, 0))
    return pl.pallas_call(
        recur_back_kernel,
        grid=(features // head,),
        in_specs=[tokens, tokens, carried, tokens, tokens, carried]
        + [tokens] * 4
        + [edge, place, tap, *gate, row],
        out_specs=[
            tokens,
            edge,
            block,
            block,
            pl.BlockSpec((taps + 4, head), lambda h: (0, h)),
        ],
        out_shape=[
            jax.ShapeDtypeStruct((batches, length, features), F32),
            jax.ShapeDtypeStruct((batches, HALO, features), F32),
            jax.ShapeDtypeStruct((features, head), BF16),
            jax.ShapeDtypeStruct((features, head), BF16),
            jax.ShapeDtypeStruct((taps + 4, features), F32),
        ],
        compiler_params=params(40),
        cost_estimate=cost(300 * batches * length * features, 50 * batches * length * features),
        name="recur_back",
    )(
        behind,
        local_grad,
        carry_back,
        running,
        local_state,
        carry,
        gate_rec,
        gate_in,
        conv,
        branch,
        halo,
        places,
        conv_w,
        gates,
        gates,
        decay_log,
    )


def units_kernel(*refs):
    normed, cots = refs[:4], refs[4:8]
    w_gate, w_up, w_down, hidden_out, gate_out, up_out, tokens, pulls = refs[8:]
    rows = normed[0].shape[0]

    @pl.when(pl.program_id(0) == 0)
    def _():
        for i in range(4):
            tokens[i * rows : (i + 1) * rows] = normed[i][...]
            pulls[i * rows : (i + 1) * rows] = cots[i][...]

    gate_pre = dot(tokens[...], w_gate[...])
    up_pre = dot(tokens[...], w_up[...])
    pulled = dot_nt(pulls[...], w_down[...])
    act, slope = gelu_pair(gate_pre)
    hidden_out[...] = (act * up_pre).astype(BF16)
    gate_out[...] = (pulled * up_pre * slope).astype(BF16)
    up_out[...] = (pulled * act).astype(BF16)


def units(normed, cots, w_gate, w_up, w_down, begin, count, tile):
    rows, width = normed[0].shape
    whole = pl.BlockSpec((rows, width), lambda j: (0, 0))
    column = pl.BlockSpec((width, tile), lambda j: (0, begin + j))
    out = pl.BlockSpec((4 * rows, tile), lambda j: (0, j))
    return pl.pallas_call(
        units_kernel,
        grid=(count,),
        in_specs=[whole] * 8
        + [column, column, pl.BlockSpec((tile, width), lambda j: (begin + j, 0))],
        out_specs=[out] * 3,
        out_shape=[jax.ShapeDtypeStruct((4 * rows, count * tile), BF16)] * 3,
        scratch_shapes=[pltpu.VMEM((4 * rows, width), BF16)] * 2,
        compiler_params=params(52),
        cost_estimate=cost(24 * rows * width * count * tile, 6 * width * count * tile),
        name="units",
    )(*normed, *cots, w_gate, w_up, w_down)


def units_back_kernel(parts, *refs):
    hidden, gate, up = refs[:parts], refs[parts : 2 * parts], refs[2 * parts : 3 * parts]
    w_gate, w_up, w_down, normed_out, ffn_out = refs[3 * parts :]
    pulled, made, start = None, None, 0
    for i in range(parts):
        span = slice(start, start + hidden[i].shape[1])
        term = dot_nt(gate[i][...], w_gate[:, span]) + dot_nt(up[i][...], w_up[:, span])
        piece = dot(hidden[i][...], w_down[span])
        pulled = term if pulled is None else pulled + term
        made = piece if made is None else made + piece
        start = span.stop
    normed_out[...] = pulled.astype(BF16)
    ffn_out[...] = made.astype(BF16)


def units_back(hidden, gate, up, w_gate, w_up, w_down):
    tile = 256
    rows = hidden[0].shape[0]
    width, held = w_gate.shape
    blocks = [pl.BlockSpec(v.shape, lambda j: (0, 0)) for v in (*hidden, *gate, *up)]
    row = pl.BlockSpec((tile, held), lambda j: (j, 0))
    out = pl.BlockSpec((rows, tile), lambda j: (0, j))
    return pl.pallas_call(
        partial(units_back_kernel, len(hidden)),
        grid=(width // tile,),
        in_specs=blocks + [row, row, pl.BlockSpec((held, tile), lambda j: (0, j))],
        out_specs=[out, out],
        out_shape=[jax.ShapeDtypeStruct((rows, width), BF16)] * 2,
        compiler_params=params(48),
        cost_estimate=cost(6 * rows * width * held, 6 * width * held),
        name="units_back",
    )(*hidden, *gate, *up, w_gate, w_up, w_down)


def token_sum(value):
    half = value.shape[0] // 2
    quarter = half // 2
    pair = value[:half].astype(F32) + swap(value[half:], WC).astype(F32)
    return pair[:quarter] + swap(pair[quarter:].astype(BF16), WX).astype(F32)


def carry_over(ends, bit, direction):
    half = ends.shape[0] // 2
    other = swap(ends, SY)
    own_run, own_end = ends[:half], ends[half:]
    oth_run, oth_end = other[:half], other[half:]
    is_last = bit if direction > 0 else 1 - bit
    ahead = pick(is_last, oth_run, own_run) * pick(is_last, own_end, oth_end)
    joined = jnp.concatenate([own_run * oth_run, ahead + pick(is_last, oth_end, own_end)], axis=0)
    entering = jnp.zeros_like(own_end)
    arrived = [shift(joined, SZ, direction * k) for k in range(1, lax.axis_size(SZ))]
    for far in reversed(arrived):
        entering = far[half:] + far[:half] * entering
    return pick(is_last, entering, oth_end + oth_run * entering)


def rows_of_eight(value):
    far = lax.axis_size(SZ)
    features, rows = value.shape
    held = [value.reshape(far, 2, 2, 2, features // (8 * far), rows)]
    for axis, place in ((WX, 2), (SY, 1), (WC, 1)):
        bit = lax.axis_index(axis)
        halves = [[lax.index_in_dim(v, i, place, keepdims=False) for i in (0, 1)] for v in held]
        mine = [pick(bit, low, high) for low, high in halves]
        sent = [pick(bit, high, low) for low, high in halves]
        got = swap(jnp.stack(sent), axis)
        held = mine + [got[i] for i in range(len(sent))]
    return jnp.concatenate([v.reshape(-1, rows) for v in held], axis=1)


def sum_of_eight(value):
    bits = [lax.axis_index(a) for a in (WC, WX, SY)]
    far = lax.axis_size(SZ)
    features, width = value.shape
    held = value.reshape(far, 2, 2, 2, features // (8 * far), width)
    for place, (bit, axis) in zip((3, 2, 1), zip(bits, (WC, WX, SY))):
        low, high = (lax.index_in_dim(held, i, place, keepdims=False) for i in (0, 1))
        got = swap(pick(bit, high, low), axis)
        held = (pick(bit, low, high).astype(F32) + got.astype(F32)).astype(BF16)
    return held.reshape(-1, width)


def eight_of(own, x_part):
    pair = jnp.concatenate([own, x_part], axis=0)
    four = jnp.concatenate([pair, swap(pair, SY)], axis=0)
    return jnp.concatenate([four, swap(four, WC)], axis=0)


def scatter_far(value):
    return lax.psum_scatter(value, SZ, scatter_dimension=0, tiled=True)


def local(
    inputs,
    positions,
    cotangent,
    gain,
    w_x,
    w_y,
    conv_w,
    conv_b,
    gate_a,
    bias_a,
    gate_i,
    bias_i,
    decay_log,
    w_out,
    gain2,
    w_gate,
    w_up,
    w_down,
):
    batches, length, features = inputs.shape
    rows = batches * length
    head = gate_a.shape[1]
    taps = conv_w.shape[0]
    held = w_gate.shape[1]
    far = lax.axis_size(SZ)
    wx, wc, sy = (lax.axis_index(a) for a in (WX, WC, SY))
    as_row = lambda v: v.reshape(1, features)
    cube = lambda v: v.reshape(batches, length, features)
    flat = lambda v: v.reshape(rows, features)

    source = flat(inputs).astype(F32)
    norm_scale = lax.rsqrt(jnp.mean(source * source, axis=-1, keepdims=True) + 1e-06)
    normed = (source * norm_scale * gain).astype(BF16)
    keep, send = split_columns(normed, wx, wc)
    recv = swap(send, WX)
    oth_x, oth_y, oth_out = swap(w_x, WC), swap(w_y, WC), swap(w_out, WC)
    gates = lax.all_gather(
        jnp.concatenate([gate_a, gate_i], axis=1), (WX, WC), axis=0, tiled=True
    )
    sent_x, own_x = project(recv, keep, w_x, oth_x)
    recv_x = swap(sent_x, WX)
    sent_y, own_y = project(recv, keep, w_y, oth_y)
    recv_y = swap(after(sent_y, recv_x), WX)

    own_x, recv_x, own_y, recv_y = cube(own_x), cube(recv_x), cube(own_y), cube(recv_y)
    edge = length - (taps - 1)
    tail = (own_x[:, edge:] + recv_x[:, edge:].astype(F32)).astype(BF16)
    halo = jnp.pad(along_seq(tail, 1).astype(F32), ((0, 0), (HALO - (taps - 1), 0), (0, 0)))
    places = positions[..., None]
    branch_x, conv, gate_rec, gate_in, running, local_state, ends = recur(
        own_x,
        recv_x,
        halo,
        places,
        conv_w,
        as_row(conv_b),
        gates,
        as_row(bias_a),
        as_row(bias_i),
        as_row(decay_log),
    )
    carry = carry_over(ends, sy, 1)[:, None]

    cot = flat(cotangent)
    cot_x = swap(after(cot, recv_y), WX)
    cots = [cot, cot_x, swap(cot, WC), swap(cot_x, WC)]
    every_cot = jnp.concatenate(cots, axis=0)

    branch_y = gelu_pair(own_y + recv_y.astype(F32))[0]
    mixed = flat(((local_state + running * carry) * branch_y).astype(BF16))
    keep, send = split_columns(mixed, wx, wc)
    sent, own = project(swap(send, WX), keep, w_out, oth_out)
    stream = source + own + swap(sent, WX).astype(F32)
    second_scale = lax.rsqrt(jnp.mean(stream * stream, axis=-1, keepdims=True) + 1e-06)
    normed_two = (stream * second_scale * gain2).astype(BF16)
    normed_x = swap(normed_two, WX)
    tokens = [normed_two, normed_x, swap(normed_two, WC), swap(normed_x, WC)]
    every_normed = jnp.concatenate(tokens, axis=0)

    def half_of_rows(value):
        turned = value.T.reshape(far, 2, features // (2 * far), -1)
        mine = pick(sy, turned[:, 0], turned[:, 1])
        got = swap(pick(sy, turned[:, 1], turned[:, 0]), SY)
        return jnp.concatenate([mine, got], axis=-1).reshape(features // 2, -1)

    cot_rows = half_of_rows(every_cot)

    tile = 384
    tiles = held // tile
    cuts = [(0, 1), (1, tiles - 1)]
    acted = [units(tokens, cots, w_gate, w_up, w_down, b, n, tile) for b, n in cuts]
    hidden, gate_grad, up_grad = zip(*acted)

    def whole_units(parts):
        got = [swap(v, SY) for v in parts]
        return [jnp.concatenate([a, b], axis=0) for a, b in zip(parts, got)]

    def far_sum(left, parts):
        return [scatter_far(dot(left, v).astype(BF16)) for v in parts]

    down_sums = far_sum(cot_rows, whole_units(hidden))
    normed_rows = half_of_rows(every_normed)

    pulled, made = units_back(hidden, gate_grad, up_grad, w_gate, w_up, w_down)
    grad_normed_two = token_sum(pulled)
    ffn_out = token_sum(made)
    output = (stream + ffn_out).astype(BF16)
    weighted_two = grad_normed_two * gain2
    grad_stream = (
        cot.astype(F32)
        + weighted_two * second_scale
        - stream * second_scale**3 * jnp.mean(weighted_two * stream, axis=-1, keepdims=True)
    )
    grad_proj = grad_stream.astype(BF16)

    whole_gate = jnp.concatenate(whole_units(gate_grad), axis=1)
    gate_sums = far_sum(normed_rows, [whole_gate])[0]
    whole_up = jnp.concatenate(whole_units(up_grad), axis=1)
    up_sums = far_sum(normed_rows, [whole_up])[0]

    proj_x = swap(grad_proj, WX)
    sent, own = project_back([(proj_x, grad_proj, w_out, oth_out)])
    grad_mixed = cube(join_columns(own, swap(sent, WX).astype(F32), wx, wc))
    grad_pre, behind, local_grad, back_ends = unroll(
        grad_mixed,
        own_y,
        recv_y,
        running,
        local_state,
        carry,
        gate_rec,
        places,
        as_row(decay_log),
        head,
    )
    carry_back = carry_over(back_ends, sy, -1)[:, None]
    spread, earlier, grad_wa, grad_wi, sums = recur_back(
        behind,
        local_grad,
        carry_back,
        running,
        local_state,
        carry,
        gate_rec,
        gate_in,
        conv,
        branch_x,
        halo,
        places,
        conv_w,
        gates,
        as_row(decay_log),
    )
    later = along_seq(earlier[:, HALO - (taps - 1) :].astype(BF16), -1).astype(F32)
    grad_branch = flat(
        (spread + jnp.pad(later, ((0, 0), (edge, 0), (0, 0)))).astype(BF16)
    )
    grad_pre = flat(grad_pre)
    pre_x, branch_grad_x = swap(grad_pre, WX), swap(grad_branch, WX)
    sent, own = project_back(
        [(branch_grad_x, grad_branch, w_x, oth_x), (pre_x, grad_pre, w_y, oth_y)]
    )
    grad_normed = join_columns(own, swap(sent, WX).astype(F32), wx, wc)
    weighted = grad_normed * gain
    input_grad = (
        grad_stream
        + weighted * norm_scale
        - source * norm_scale**3 * jnp.mean(weighted * source, axis=-1, keepdims=True)
    )

    normed_eight = rows_of_eight(normed.T)
    mixed_eight = rows_of_eight(mixed.T)
    out_sums = scatter_far(dot(mixed_eight, eight_of(grad_proj, proj_x)).astype(BF16))
    y_sums = scatter_far(dot(normed_eight, eight_of(grad_pre, pre_x)).astype(BF16))
    x_sums = scatter_far(dot(normed_eight, eight_of(grad_branch, branch_grad_x)).astype(BF16))
    small = jnp.concatenate(
        [
            jnp.sum(grad_normed * source * norm_scale, axis=0)[None],
            jnp.sum(grad_normed_two * stream * second_scale, axis=0)[None],
            sums,
        ],
        axis=0,
    )
    small = jnp.pad(small.T, ((0, 0), (0, 128 - small.shape[0]))).astype(BF16)
    rest = scatter_far(
        sum_of_eight(jnp.concatenate([grad_wa, grad_wi, small], axis=1))
    ).astype(F32)
    grads = rest[:, 2 * head :]
    return (
        cube(output),
        cube(input_grad),
        grads[:, 0],
        x_sums.astype(F32),
        y_sums.astype(F32),
        grads[:, 2 : 2 + taps].T,
        grads[:, 2 + taps],
        rest[:, :head],
        grads[:, 3 + taps],
        rest[:, head : 2 * head],
        grads[:, 4 + taps],
        grads[:, 5 + taps],
        out_sums.astype(F32),
        grads[:, 1],
        gate_sums.astype(F32),
        up_sums.astype(F32),
        jnp.concatenate([v.T for v in down_sums], axis=0).astype(F32),
    )


def solution(mesh):
    seq, wt = mesh.devices.shape
    split = Mesh(mesh.devices.reshape(seq // 2, 2, wt // 2, 2), (SZ, SY, WX, WC))
    s, w = (SZ, SY), (WX, WC)
    everywhere = (SZ, SY, WX, WC)
    return jax.shard_map(
        local,
        mesh=split,
        in_specs=(
            P(w, s, None),
            P(w, s),
            P(w, s, None),
            P(),
            P(w, None),
            P(w, None),
            P(),
            P(),
            P(w, None),
            P(),
            P(w, None),
            P(),
            P(),
            P(w, None),
            P(),
            P(None, w),
            P(None, w),
            P(w, None),
        ),
        out_specs=(
            P(w, s, None),
            P(w, s, None),
            P(everywhere),
            P(everywhere, None),
            P(everywhere, None),
            P(None, everywhere),
            P(everywhere),
            P(everywhere, None),
            P(everywhere),
            P(everywhere, None),
            P(everywhere),
            P(everywhere),
            P(everywhere, None),
            P(everywhere),
            P(s, w),
            P(s, w),
            P(w, s),
        ),
        check_vma=False,
    )
```

```python
from functools import partial

import jax
import jax.numpy as jnp
from jax import lax
from jax.experimental import pallas as pl
from jax.experimental.pallas import tpu as pltpu
from jax.sharding import Mesh
from jax.sharding import PartitionSpec as P

SZ, SY, WX, WC = ("sz", "sy", "wx", "wc")
F32, BF16 = (jnp.float32, jnp.bfloat16)
HALO = 8
ROOT_2_PI = 0.7978845608028654
CUBIC = 0.044715
VMEM_GRANT = 58 << 20
COST_SHARE = 0.02
HEADS_EACH = 2


def swap(value, axis):
    return lax.ppermute(value, axis, [(0, 1), (1, 0)])


def shift(value, axis, steps):
    count = lax.axis_size(axis)
    initial, last = (max(0, -steps), min(count, count - steps))
    return lax.ppermute(value, axis, [(source, source + steps) for source in range(initial, last)])


def around(value, steps):
    count = lax.axis_size(SZ)
    return lax.ppermute(value, SZ, [((to + steps) % count, to) for to in range(count)])


def partner_far(value):
    count = lax.axis_size(SZ)
    return lax.ppermute(value, SZ, [(source, source ^ 1) for source in range(count)])


def along_seq(value, steps):
    count = lax.axis_size(SZ) * lax.axis_size(SY)
    initial, last = (max(0, -steps), min(count, count - steps))
    return lax.ppermute(
        value, (SZ, SY), [(source, source + steps) for source in range(initial, last)]
    )


def pick(bit, zero, one):
    return jnp.where(bit == 0, zero, one)


def after(value, *others):
    return lax.optimization_barrier((value, *others))[0]


def tie(*values):
    return lax.optimization_barrier(values)


class Line:
    def __init__(self):
        self.last = None

    def __call__(self, *values):
        if self.last is None:
            return values
        return lax.optimization_barrier((*values, self.last))[:-1]

    def mark(self, value):
        self.last = value
        return value


def gelu_pair(value):
    square = value * value
    tanh = jnp.tanh(ROOT_2_PI * value * (1.0 + CUBIC * square))
    half = 0.5 * (1.0 + tanh)
    slope = half + 0.5 * value * (1.0 - tanh * tanh) * (
        ROOT_2_PI * (1.0 + 3.0 * CUBIC * square)
    )
    return value * half, slope


def dot(left, right):
    return jnp.dot(left, right, preferred_element_type=F32)


def dot_nt(left, right):
    return lax.dot_general(left, right, (((1,), (1,)), ((), ())), preferred_element_type=F32)


def dot_tn(left, right):
    return lax.dot_general(left, right, (((0,), (0,)), ((), ())), preferred_element_type=F32)


def params():
    return pltpu.CompilerParams(
        dimension_semantics=("arbitrary",), vmem_limit_bytes=VMEM_GRANT
    )


def cost(flops, nbytes):
    return pl.CostEstimate(
        flops=int(flops * COST_SHARE), bytes_accessed=int(nbytes * COST_SHARE), transcendentals=0
    )


def split_columns(value, wx, wc):
    quarter = value.shape[-1] // 4
    parts = [value[..., i * quarter : (i + 1) * quarter] for i in range(4)]
    near = [pick(wx, parts[0], parts[2]), pick(wx, parts[1], parts[3])]
    far = [pick(wx, parts[2], parts[0]), pick(wx, parts[3], parts[1])]
    keep = jnp.concatenate([pick(wc, near[0], near[1]), pick(wc, near[1], near[0])], axis=-1)
    send = jnp.concatenate([pick(wc, far[0], far[1]), pick(wc, far[1], far[0])], axis=-1)
    return keep, send


def join_columns(near, far, wx, wc):
    near = [pick(wc, near[0], near[1]), pick(wc, near[1], near[0])]
    far = [pick(wc, far[0], far[1]), pick(wc, far[1], far[0])]
    return jnp.concatenate(
        [
            pick(wx, near[0], far[0]),
            pick(wx, near[1], far[1]),
            pick(wx, far[0], near[0]),
            pick(wx, far[1], near[1]),
        ],
        axis=-1,
    )


def project(recv, keep, w_own, w_oth):
    rows = recv.shape[0]
    left = jnp.concatenate([recv, keep], axis=0)
    total = dot(left, jnp.concatenate([w_own, w_oth], axis=0))
    return total[:rows].astype(BF16), total[rows:]


def project_back(terms):
    rows = terms[0][0].shape[0]
    total = 0.0
    for recv, own, w_own, w_oth in terms:
        left = jnp.concatenate([recv, own], axis=0)
        total = total + dot_nt(left, jnp.concatenate([w_own, w_oth], axis=0))
    half = total.shape[1] // 2
    total = jnp.stack([total[:, :half], total[:, half:]])
    return total[:, :rows].astype(BF16), total[:, rows:]


def less_one_exp(value):
    series = 1.0
    for n in (9, 8, 7, 6, 5, 4, 3, 2):
        series = 1.0 + value * (1.0 / n) * series
    return jnp.where(value > -0.5, -value * series, 1.0 - jnp.exp(value))


def shifted_down(value, steps, fill):
    edge = jnp.full((value.shape[0], steps, value.shape[2]), fill, F32)
    return jnp.concatenate([edge, value[:, : value.shape[1] - steps]], axis=1)


def shifted_up(value, steps, fill):
    edge = jnp.full((value.shape[0], steps, value.shape[2]), fill, F32)
    return jnp.concatenate([value[:, steps:], edge], axis=1)


def scan_rows(decay, driven, mover):
    steps = 1
    while steps < decay.shape[1]:
        driven = driven + decay * mover(driven, steps, 0.0)
        decay = decay * mover(decay, steps, 1.0)
        steps *= 2
    return decay, driven


def tap_mask(places, offset):
    return (places >= offset).astype(F32)


def by_head(flat, gate, product):
    head = gate.shape[1]
    spans = [slice(i, i + head) for i in range(0, flat.shape[1], head)]
    return jnp.concatenate([product(flat[:, s], gate[s]) for s in spans], axis=1)


def recur_kernel(
    own,
    recv,
    halo,
    places,
    conv_w,
    conv_b,
    gate_a,
    gate_i,
    bias_a,
    bias_i,
    decay_log,
    branch_out,
    conv_out,
    rec_out,
    in_out,
    run_out,
    state_out,
    ends_out,
):
    batches, length, width = own.shape
    branch = (own[...] + recv[...].astype(F32)).astype(BF16)
    branch_out[...] = branch
    extended = jnp.concatenate([halo[...], branch.astype(F32)], axis=1)
    spot = places[...]
    total = jnp.zeros((batches, length, width), F32) + conv_b[...][None]
    for offset in range(conv_w.shape[0]):
        moved = extended[:, HALO - offset : HALO - offset + length]
        total = total + conv_w[offset : offset + 1][None] * moved * tap_mask(spot, offset)
    conv = total.astype(BF16)
    conv_out[...] = conv
    flat = conv.reshape(batches * length, width)
    shape = (batches, length, width)
    gate_rec = jax.nn.sigmoid(by_head(flat, gate_a, dot) + bias_a[...]).reshape(shape)
    gate_in = jax.nn.sigmoid(by_head(flat, gate_i, dot) + bias_i[...]).reshape(shape)
    rec_out[...] = gate_rec
    in_out[...] = gate_in
    log_a = -8.0 * gate_rec * jnp.exp(decay_log[...])[None]
    alive = tap_mask(spot, 1)
    root = jnp.sqrt(less_one_exp(2.0 * log_a))
    multiplier = alive * root + (1.0 - alive)
    decay = jnp.exp(log_a) * alive
    driven = conv.astype(F32) * gate_in * multiplier
    running, state = scan_rows(decay, driven, shifted_down)
    run_out[...] = running
    state_out[...] = state
    for b in range(batches):
        ends_out[b : b + 1] = running[b, length - 1 :]
        ends_out[batches + b : batches + b + 1] = state[b, length - 1 :]


def head_specs(batches, length, head, taps, group=1):
    head = head * group
    tokens = pl.BlockSpec((batches, length, head), lambda h: (0, 0, h))
    edge = pl.BlockSpec((batches, HALO, head), lambda h: (0, 0, h))
    place = pl.BlockSpec((batches, length, 1), lambda h: (0, 0, 0))
    row = pl.BlockSpec((1, head), lambda h: (0, h))
    tap = pl.BlockSpec((taps, head), lambda h: (0, h))
    gates = [
        pl.BlockSpec((head, head // group), lambda h: (h, 0)),
        pl.BlockSpec((head, head // group), lambda h: (h, 1)),
    ]
    ends = pl.BlockSpec((2 * batches, head), lambda h: (0, h))
    carry = pl.BlockSpec((batches, 1, head), lambda h: (0, 0, h))
    return tokens, edge, place, row, tap, gates, ends, carry


def recur(own, recv, halo, places, conv_w, conv_b, gates, bias_a, bias_i, decay_log):
    batches, length, features = own.shape
    head = gates.shape[1] // 2
    tokens, edge, place, row, tap, gate, ends, _ = head_specs(
        batches, length, head, conv_w.shape[0], HEADS_EACH
    )
    full = lambda dtype: jax.ShapeDtypeStruct((batches, length, features), dtype)
    return pl.pallas_call(
        recur_kernel,
        grid=(features // (head * HEADS_EACH),),
        in_specs=[tokens, tokens, edge, place, tap, row, *gate, row, row, row],
        out_specs=[tokens] * 6 + [ends],
        out_shape=[full(BF16), full(BF16)]
        + [full(F32)] * 4
        + [jax.ShapeDtypeStruct((2 * batches, features), F32)],
        compiler_params=params(),
        cost_estimate=cost(200 * batches * length * features, 40 * batches * length * features),
        name="recur",
    )(own, recv, halo, places, conv_w, conv_b, gates, gates, bias_a, bias_i, decay_log)


def unroll_kernel(
    mixed_grad,
    own_y,
    recv_y,
    running,
    local_state,
    carry,
    gate_rec,
    places,
    decay_log,
    pre_out,
    behind_out,
    local_out,
    ends_out,
):
    batches, length, _ = mixed_grad.shape
    pulled = mixed_grad[...].astype(F32)
    branch_y, slope = gelu_pair(own_y[...] + recv_y[...].astype(F32))
    state = local_state[...] + running[...] * carry[...]
    pre_out[...] = (pulled * state * slope).astype(BF16)
    log_a = -8.0 * gate_rec[...] * jnp.exp(decay_log[...])[None]
    decay = jnp.exp(log_a) * tap_mask(places[...], 1)
    following = shifted_up(decay, 1, 1.0)
    behind, local = scan_rows(following, pulled * branch_y, shifted_up)
    behind_out[...] = behind
    local_out[...] = local
    for b in range(batches):
        ends_out[b : b + 1] = running[b, length - 1 :, :]
        ends_out[batches + b : batches + b + 1] = decay[b, :1] * local[b, :1]


def unroll(mixed_grad, own_y, recv_y, running, local_state, carry, gate_rec, places, decay_log, head):
    batches, length, features = mixed_grad.shape
    tokens, _, place, row, _, _, ends, carried = head_specs(batches, length, head, 1, HEADS_EACH)
    full = lambda dtype: jax.ShapeDtypeStruct((batches, length, features), dtype)
    return pl.pallas_call(
        unroll_kernel,
        grid=(features // (head * HEADS_EACH),),
        in_specs=[tokens] * 5 + [carried, tokens, place, row],
        out_specs=[tokens] * 3 + [ends],
        out_shape=[full(BF16), full(F32), full(F32)]
        + [jax.ShapeDtypeStruct((2 * batches, features), F32)],
        compiler_params=params(),
        cost_estimate=cost(200 * batches * length * features, 40 * batches * length * features),
        name="unroll",
    )(mixed_grad, own_y, recv_y, running, local_state, carry, gate_rec, places, decay_log)


def recur_back_kernel(
    behind,
    local_grad,
    carry_back,
    running,
    local_state,
    carry,
    gate_rec,
    gate_in,
    conv,
    branch,
    halo,
    places,
    conv_w,
    gate_a,
    gate_i,
    decay_log,
    spread_out,
    earlier_out,
    wa_out,
    wi_out,
    sums_out,
):
    batches, length, width = behind.shape
    shape = (batches, length, width)
    rows = batches * length
    spot = places[...]
    alive = tap_mask(spot, 1)
    rate = jnp.exp(decay_log[...])[None]
    rec, inner = gate_rec[...], gate_in[...]
    log_a = -8.0 * rec * rate
    raw = jnp.exp(log_a)
    root = jnp.sqrt(less_one_exp(2.0 * log_a))
    multiplier = alive * root + (1.0 - alive)
    conv_low = conv[...]
    conv_full = conv_low.astype(F32)
    grad_state = local_grad[...] + behind[...] * carry_back[...]
    state = local_state[...] + running[...] * carry[...]
    before = jnp.concatenate([carry[...], state[:, : length - 1]], axis=1)
    scaled = grad_state * conv_full * inner
    grad_log = alive * raw * (grad_state * before - scaled * raw / root)
    grad_a = grad_log * (-8.0 * rate) * rec * (1.0 - rec)
    grad_i = scaled * multiplier * (1.0 - inner)
    low_a = grad_a.astype(BF16).reshape(rows, width)
    low_i = grad_i.astype(BF16).reshape(rows, width)
    pulled = grad_state * inner * multiplier
    pulled = pulled + (
        by_head(low_a, gate_a, dot_nt) + by_head(low_i, gate_i, dot_nt)
    ).reshape(shape)
    pulled = pulled.astype(BF16).astype(F32)
    flat = conv_low.reshape(rows, width)
    head = gate_a.shape[1]
    for i in range(0, width, head):
        span = slice(i, i + head)
        wa_out[span] = dot_tn(flat[:, span], low_a[:, span]).astype(BF16)
        wi_out[span] = dot_tn(flat[:, span], low_i[:, span]).astype(BF16)
    extended = jnp.concatenate([halo[...], branch[...].astype(F32)], axis=1)
    taps = conv_w.shape[0]
    spread = jnp.zeros((batches, length + HALO, width), F32)
    blank = jnp.zeros((batches, HALO, width), F32)
    sums = []
    add = lambda value: jnp.sum(value.reshape(rows, width), axis=0, keepdims=True)
    for offset in range(taps):
        masked = pulled * tap_mask(spot, offset)
        weighted = jnp.concatenate([blank, conv_w[offset : offset + 1][None] * masked], axis=1)
        spread = spread + (shifted_up(weighted, offset, 0.0) if offset else weighted)
        sums.append(add(masked * extended[:, HALO - offset : HALO - offset + length]))
    earlier_out[...] = spread[:, :HALO]
    spread_out[...] = spread[:, HALO:]
    sums += [add(pulled), add(grad_a), add(grad_i), add(grad_log * log_a)]
    sums_out[...] = jnp.concatenate(sums, axis=0)


def recur_back(
    behind,
    local_grad,
    carry_back,
    running,
    local_state,
    carry,
    gate_rec,
    gate_in,
    conv,
    branch,
    halo,
    places,
    conv_w,
    gates,
    decay_log,
):
    batches, length, features = behind.shape
    head = gates.shape[1] // 2
    taps = conv_w.shape[0]
    tokens, edge, place, row, tap, gate, _, carried = head_specs(
        batches, length, head, taps, HEADS_EACH
    )
    block = pl.BlockSpec((head * HEADS_EACH, head), lambda h: (h, 0))
    return pl.pallas_call(
        recur_back_kernel,
        grid=(features // (head * HEADS_EACH),),
        in_specs=[tokens, tokens, carried, tokens, tokens, carried]
        + [tokens] * 4
        + [edge, place, tap, *gate, row],
        out_specs=[
            tokens,
            edge,
            block,
            block,
            pl.BlockSpec((taps + 4, head * HEADS_EACH), lambda h: (0, h)),
        ],
        out_shape=[
            jax.ShapeDtypeStruct((batches, length, features), F32),
            jax.ShapeDtypeStruct((batches, HALO, features), F32),
            jax.ShapeDtypeStruct((features, head), BF16),
            jax.ShapeDtypeStruct((features, head), BF16),
            jax.ShapeDtypeStruct((taps + 4, features), F32),
        ],
        compiler_params=params(),
        cost_estimate=cost(300 * batches * length * features, 50 * batches * length * features),
        name="recur_back",
    )(
        behind,
        local_grad,
        carry_back,
        running,
        local_state,
        carry,
        gate_rec,
        gate_in,
        conv,
        branch,
        halo,
        places,
        conv_w,
        gates,
        gates,
        decay_log,
    )


def unit_step(gate_pre, up_pre, pulled, hidden_out, gate_out, up_out):
    act, slope = gelu_pair(gate_pre)
    hidden_out[...] = (act * up_pre).astype(BF16)
    gate_out[...] = (pulled * up_pre * slope).astype(BF16)
    up_out[...] = (pulled * act).astype(BF16)


def fill(target, pieces):
    start = 0
    for piece in pieces:
        target[start : start + piece.shape[0]] = piece
        start += piece.shape[0]


def units_kernel(count, *refs):
    pieces, (w_gate, w_up, pulled, hidden_out, gate_out, up_out, tokens) = refs[:count], refs[count:]

    @pl.when(pl.program_id(0) == 0)
    def _():
        fill(tokens, [p[...] for p in pieces])

    gate_pre, up_pre = dot(tokens[...], w_gate[...]), dot(tokens[...], w_up[...])
    unit_step(gate_pre, up_pre, pulled[...].astype(F32), hidden_out, gate_out, up_out)


def units(pieces, w_gate, w_up, pulled):
    count = len(pieces)
    rows, width = pieces[0].shape
    held = w_gate.shape[1]
    tile = 640
    whole = pl.BlockSpec((rows, width), lambda j: (0, 0), pipeline_mode=pl.Buffered(1))
    column = pl.BlockSpec((width, tile), lambda j: (0, j))
    out = pl.BlockSpec((count * rows, tile), lambda j: (0, j))
    return pl.pallas_call(
        partial(units_kernel, count),
        grid=(held // tile,),
        in_specs=[whole] * count + [column, column, out],
        out_specs=[out] * 3,
        out_shape=[jax.ShapeDtypeStruct((count * rows, held), BF16)] * 3,
        scratch_shapes=[pltpu.VMEM((count * rows, width), BF16)],
        compiler_params=params(),
        cost_estimate=cost(4 * count * rows * width * held, 4 * width * held),
        name="units",
    )(*pieces, w_gate, w_up, pulled)


def pull_units_kernel(count, *refs):
    pieces, (w_down, out, tokens) = refs[:count], refs[count:]

    @pl.when(pl.program_id(0) == 0)
    def _():
        fill(tokens, [p[...] for p in pieces])

    out[...] = dot_nt(tokens[...], w_down[...]).astype(BF16)


def pull_units(pieces, w_down):
    count = len(pieces)
    rows, width = pieces[0].shape
    held = w_down.shape[0]
    tile = 640
    whole = pl.BlockSpec((rows, width), lambda j: (0, 0), pipeline_mode=pl.Buffered(1))
    return pl.pallas_call(
        partial(pull_units_kernel, count),
        grid=(held // tile,),
        in_specs=[whole] * count + [pl.BlockSpec((tile, width), lambda j: (j, 0))],
        out_specs=pl.BlockSpec((count * rows, tile), lambda j: (0, j)),
        out_shape=jax.ShapeDtypeStruct((count * rows, held), BF16),
        scratch_shapes=[pltpu.VMEM((count * rows, width), BF16)],
        compiler_params=params(),
        cost_estimate=cost(2 * count * rows * width * held, 2 * width * held),
        name="pull_units",
    )(*pieces, w_down)


def units_back_kernel(gate, up, w_gate, w_up, out):
    out[...] = (dot_nt(gate[...], w_gate[...]) + dot_nt(up[...], w_up[...])).astype(BF16)


def units_back(gate, up, w_gate, w_up):
    tile = 640
    rows = gate.shape[0]
    width, held = w_gate.shape
    whole = pl.BlockSpec((rows, held), lambda j: (0, 0), pipeline_mode=pl.Buffered(1))
    row = pl.BlockSpec((tile, held), lambda j: (j, 0))
    return pl.pallas_call(
        units_back_kernel,
        grid=(width // tile,),
        in_specs=[whole, whole, row, row],
        out_specs=pl.BlockSpec((rows, tile), lambda j: (0, j)),
        out_shape=jax.ShapeDtypeStruct((rows, width), BF16),
        compiler_params=params(),
        cost_estimate=cost(4 * rows * width * held, 4 * width * held),
        name="units_back",
    )(gate, up, w_gate, w_up)


def units_made_kernel(hidden, w_down, out):
    out[...] = dot(hidden[...], w_down[...]).astype(BF16)


def units_made(hidden, w_down):
    tile = 1280
    rows, held = hidden.shape
    width = w_down.shape[1]
    return pl.pallas_call(
        units_made_kernel,
        grid=(width // tile,),
        in_specs=[
            pl.BlockSpec((rows, held), lambda j: (0, 0), pipeline_mode=pl.Buffered(1)),
            pl.BlockSpec((held, tile), lambda j: (0, j)),
        ],
        out_specs=pl.BlockSpec((rows, tile), lambda j: (0, j)),
        out_shape=jax.ShapeDtypeStruct((rows, width), BF16),
        compiler_params=params(),
        cost_estimate=cost(2 * rows * width * held, 2 * width * held),
        name="units_made",
    )(hidden, w_down)


def window_of(held):
    width = -(-held // 2 // 128) * 128
    return width, held - width


def others(places, gathered, pieces):
    count = len(pieces)
    return [gathered[(places[0] + j) % (count + 1)] for j in range(1, count + 1)] + [
        p[...] for p in pieces
    ]


def share_pull_kernel(count, places, *refs):
    gathered, pieces, (w_down, out, tokens) = refs[0], refs[1 : 1 + count], refs[1 + count :]

    @pl.when(pl.program_id(0) == 0)
    def _():
        fill(tokens, others(places, gathered, pieces))

    out[...] = dot_nt(tokens[...], w_down[...]).astype(BF16)


def share_kernel(count, places, *refs):
    gathered, pieces = refs[0], refs[1 : 1 + count]
    w_gate, w_up, pulled, hidden_out, gate_out, up_out, tokens = refs[1 + count :]

    @pl.when(pl.program_id(0) == 0)
    def _():
        fill(tokens, others(places, gathered, pieces))

    gate_pre, up_pre = dot(tokens[...], w_gate[...]), dot(tokens[...], w_up[...])
    unit_step(gate_pre, up_pre, pulled[...].astype(F32), hidden_out, gate_out, up_out)


def share_call(kernel, places, gathered, pieces, weights, more, outs, name):
    count = len(pieces)
    rows, width = pieces[0].shape
    tile = 512
    held = weights[0].shape[0] if weights[0].shape[1] == width else weights[0].shape[1]
    window, offset = window_of(held)
    total = 2 * count * rows
    specs = []
    for weight in weights:
        if weight.shape[1] == width:
            specs.append(
                pl.BlockSpec(
                    (pl.Element(tile), pl.Element(width)),
                    lambda j, places: (pl.multiple_of(places[1] * offset + j * tile, 128), 0),
                )
            )
        else:
            specs.append(
                pl.BlockSpec(
                    (pl.Element(width), pl.Element(tile)),
                    lambda j, places: (0, pl.multiple_of(places[1] * offset + j * tile, 128)),
                )
            )
    out = pl.BlockSpec((total, tile), lambda j, places: (0, j))
    result = pl.pallas_call(
        partial(kernel, count),
        grid_spec=pltpu.PrefetchScalarGridSpec(
            num_scalar_prefetch=1,
            grid=(window // tile,),
            in_specs=[
                pl.BlockSpec(
                    gathered.shape, lambda j, places: (0, 0, 0), pipeline_mode=pl.Buffered(1)
                )
            ]
            + [
                pl.BlockSpec((rows, width), lambda j, places: (0, 0), pipeline_mode=pl.Buffered(1))
            ]
            * count
            + specs
            + [out] * len(more),
            out_specs=[out] * outs,
            scratch_shapes=[pltpu.VMEM((total, width), BF16)],
        ),
        out_shape=[jax.ShapeDtypeStruct((total, window), BF16)] * outs,
        compiler_params=params(),
        cost_estimate=cost(
            2 * len(weights) * total * width * window, 2 * len(weights) * width * window
        ),
        name=name,
    )(places, gathered, *pieces, *weights, *more)
    return result


def share_pull(places, gathered, pieces, w_down):
    return share_call(share_pull_kernel, places, gathered, pieces, [w_down], [], 1, "share_pull")[0]


def share(places, gathered, pieces, w_gate, w_up, pulled):
    return share_call(
        share_kernel, places, gathered, pieces, [w_gate, w_up], [pulled], 3, "share"
    )


def unit_grad_kernel(count, kinds, places, *refs):
    token_refs, refs = refs[: 2 * (1 + count)], refs[2 * (1 + count) :]
    own_x, acts, outs = refs[:2], refs[2 : 2 + 3 * kinds], refs[2 + 3 * kinds : 2 + 5 * kinds]
    left, whole = refs[2 + 5 * kinds :]
    block = whole.shape[0] // 2
    here, there = token_refs[: 1 + count], token_refs[1 + count :]
    me = places[0]
    fill(
        left,
        [here[0][me], there[0][me], own_x[0][...], own_x[1][...]]
        + others(places, here[0], here[1:])
        + others(places, there[0], there[1:]),
    )
    own = pl.multiple_of(places[2] * block, block)
    other = pl.multiple_of((1 - places[2]) * block, block)
    for kind in range(kinds):
        parts = acts[3 * kind : 3 * kind + 3]
        total, start = None, 0
        for part in parts:
            size = part.shape[0]
            term = dot_tn(left[start : start + size], part[...])
            total = term if total is None else total + term
            start += size
        whole[...] = total
        outs[2 * kind][0] = whole[pl.ds(own, block)]
        outs[2 * kind + 1][0] = whole[pl.ds(other, block)].astype(BF16)


def unit_grad(places, here, there, own_x, acts):
    count, kinds = len(here[1]), len(acts)
    rows, features = own_x[0].shape
    window, offset = window_of(acts[0][0].shape[1])
    width = features // (count + 1)
    total = 4 * (count + 1) * rows
    once = pl.Buffered(1)
    gathered = pl.BlockSpec((count + 1, rows, width), lambda i, p: (0, 0, 2 * (p[0] // 2) + i))
    piece = pl.BlockSpec((rows, width), lambda i, p: (0, 2 * (p[0] // 2) + i))
    mine = pl.BlockSpec(
        (pl.Element(4 * rows), pl.Element(window)),
        lambda i, p: (0, pl.multiple_of(p[1] * offset, 128)),
        pipeline_mode=once,
    )
    act = pl.BlockSpec((2 * count * rows, window), lambda i, p: (0, 0), pipeline_mode=once)
    out = pl.BlockSpec((1, width // 2, window), lambda i, p: (i, 0, 0))
    shape = (2, width // 2, window)
    return pl.pallas_call(
        partial(unit_grad_kernel, count, kinds),
        grid_spec=pltpu.PrefetchScalarGridSpec(
            num_scalar_prefetch=1,
            grid=(2,),
            in_specs=([gathered] + [piece] * count) * 2 + [piece] * 2 + [mine, act, act] * kinds,
            out_specs=[out] * (2 * kinds),
            scratch_shapes=[
                pltpu.VMEM((total, width), BF16),
                pltpu.VMEM((width, window), F32),
            ],
        ),
        out_shape=[jax.ShapeDtypeStruct(shape, d) for d in (F32, BF16)] * kinds,
        compiler_params=params(),
        cost_estimate=cost(4 * kinds * total * width * window, 2 * kinds * total * window),
        name="unit_grad",
    )(places, here[0], *here[1], there[0], *there[1], *own_x, *[a for v in acts for a in v])


def window_part(value, places, axis):
    window, offset = window_of(value.shape[axis])
    return lax.dynamic_slice_in_dim(value, places[1] * offset, window, axis=axis)


def others_plain(places, gathered, pieces):
    count = len(pieces)
    rolled = jnp.roll(gathered, -places[0], axis=0)[1:].reshape(-1, gathered.shape[2])
    return jnp.concatenate([rolled, *pieces], axis=0)


def share_pull_plain(places, gathered, pieces, w_down):
    tokens = others_plain(places, gathered, pieces)
    return dot_nt(tokens, window_part(w_down, places, 0)).astype(BF16)


def share_plain(places, gathered, pieces, w_gate, w_up, pulled):
    tokens = others_plain(places, gathered, pieces)
    act, slope = gelu_pair(dot(tokens, window_part(w_gate, places, 1)))
    up_pre = dot(tokens, window_part(w_up, places, 1))
    pulled = pulled.astype(F32)
    return [v.astype(BF16) for v in (act * up_pre, pulled * up_pre * slope, pulled * act)]


def unit_grad_plain(places, here, there, own_x, acts):
    features = own_x[0].shape[1]
    block = features // (2 * (len(here[1]) + 1))
    at = lambda v: lax.dynamic_index_in_dim(v, places[0], 0, keepdims=False)
    tokens = [at(here[0]), at(there[0]), *own_x]
    tokens = jnp.concatenate(
        tokens + [others_plain(places, *here), others_plain(places, *there)], axis=0
    )
    tokens = lax.dynamic_slice_in_dim(tokens, places[0] // 2 * 4 * block, 4 * block, axis=1)
    outs = []
    for own, *rest in acts:
        right = jnp.concatenate([window_part(own, places, 1), *rest], axis=0)
        whole = dot_tn(tokens, right).reshape(2, 2, block, -1)
        outs.append(pick(places[2], whole[:, 0], whole[:, 1]))
        outs.append(pick(places[2], whole[:, 1], whole[:, 0]).astype(BF16))
    return outs


def carry_join(ends, other, bit, direction):
    half = ends.shape[0] // 2
    is_last = bit if direction > 0 else 1 - bit
    first_end = pick(is_last, ends[half:], other[half:])
    last_end = pick(is_last, other[half:], ends[half:])
    last_run = pick(is_last, other[:half], ends[:half])
    return jnp.concatenate(
        [ends[:half] * other[:half], last_run * first_end + last_end], axis=0
    )


def carry_shifts(joined, direction):
    return [shift(joined, SZ, direction * k) for k in range(1, lax.axis_size(SZ))]


def line_tree(line, *values):
    leaves, tree = jax.tree.flatten(values)
    return jax.tree.unflatten(tree, line(*leaves))


def tied_carry(line, other, arrived):
    other, *arrived = line(other, *arrived)
    return other, arrived


def carry_finish(other, arrived, bit, direction):
    half = other.shape[0] // 2
    is_last = bit if direction > 0 else 1 - bit
    entering = jnp.zeros_like(other[half:])
    for far in reversed(arrived):
        entering = far[half:] + far[:half] * entering
    return pick(is_last, entering, other[half:] + other[:half] * entering)[:, None]


def rows_for(axis, place, stack):
    bit = lax.axis_index(axis)
    low, high = (lax.index_in_dim(stack, i, place, keepdims=False) for i in (0, 1))
    return pick(bit, low, high), pick(bit, high, low)


def token_grad_kernel(offset, *refs):
    pieces, (near, away, out, left, right) = refs[:8], refs[8:]
    rows = pieces[0].shape[0]

    @pl.when(pl.program_id(0) == 0)
    def _():
        for i in range(8):
            held = (near if i < 4 else away)[i % 4]
            left[:, i * rows : (i + 1) * rows] = held[:, offset : offset + rows]

    fill(right, [p[...] for p in pieces])
    out[...] = dot(left[...], right[...]).astype(BF16)


def token_grad(near, away, second, pieces):
    rows, width = pieces[0].shape
    held = near.shape[1]
    tile = 640
    piece = pl.BlockSpec((rows, tile), lambda j: (0, j))
    whole = pl.BlockSpec(near.shape, lambda j: (0, 0, 0), pipeline_mode=pl.Buffered(1))
    return pl.pallas_call(
        partial(token_grad_kernel, second * rows),
        grid=(width // tile,),
        in_specs=[piece] * 8 + [whole, whole],
        out_specs=pl.BlockSpec((held, tile), lambda j: (0, j)),
        out_shape=jax.ShapeDtypeStruct((held, width), BF16),
        scratch_shapes=[pltpu.VMEM((held, 8 * rows), BF16), pltpu.VMEM((8 * rows, tile), BF16)],
        compiler_params=params(),
        cost_estimate=cost(16 * held * rows * width, 20 * rows * width),
        name="token_grad",
    )(*pieces, near, away)


def total_of_all(value):
    far = lax.axis_size(SZ)
    held = value.reshape(far, 2, 2, 2, -1)
    for place, axis in ((3, WC), (2, WX), (1, SY)):
        bit = lax.axis_index(axis)
        low, high = (lax.index_in_dim(held, i, place, keepdims=False) for i in (0, 1))
        held = pick(bit, low, high) + swap(pick(bit, high, low), axis)
    here = lax.axis_index(SZ)
    mine = lax.dynamic_index_in_dim(held, here, 0, keepdims=False)
    for steps in range(1, far):
        block = lax.dynamic_index_in_dim(held, (here - steps) % far, 0, keepdims=False)
        mine = mine + around(block, steps)
    return mine


def join_gates(own, core, x_part, both, wx, wc):
    parts = [[pick(wc, p, q), pick(wc, q, p)] for p, q in ((own, core), (x_part, both))]
    return jnp.concatenate(
        [pick(wx, parts[0][i], parts[1][i]) for i in (0, 1)]
        + [pick(wx, parts[1][i], parts[0][i]) for i in (0, 1)],
        axis=0,
    )


def scatter_far(value):
    return lax.psum_scatter(value, SZ, scatter_dimension=0, tiled=True)


def local(
    inputs,
    positions,
    cotangent,
    gain,
    w_x,
    w_y,
    conv_w,
    conv_b,
    gate_a,
    bias_a,
    gate_i,
    bias_i,
    decay_log,
    w_out,
    gain2,
    w_gate,
    w_up,
    w_down,
):
    batches, length, features = inputs.shape
    rows = batches * length
    head = gate_a.shape[1]
    taps = conv_w.shape[0]
    held = w_gate.shape[1]
    far = lax.axis_size(SZ)
    wx, wc, sy = (lax.axis_index(a) for a in (WX, WC, SY))
    as_row = lambda v: v.reshape(1, features)
    cube = lambda v: v.reshape(batches, length, features)
    flat = lambda v: v.reshape(rows, features)

    line = Line()
    sz = lax.axis_index(SZ)
    parity = sz % 2
    spots = jnp.stack([sz, parity, sy]).astype(jnp.int32)
    edge = length - (taps - 1)
    places = positions[..., None]
    half = 2 * rows
    low = lambda v: v.astype(BF16)
    wide = lambda v: v.astype(F32)
    plain = (features // far) % 128 != 0 or far > 4
    pull_of, share_of, grad_of = (
        (share_pull_plain, share_plain, unit_grad_plain) if plain else (share_pull, share, unit_grad)
    )

    oth_x, oth_y, oth_out = swap(w_x, WC), swap(w_y, WC), swap(w_out, WC)
    own_gates = jnp.concatenate([gate_a, gate_i], axis=1)
    gates = lax.all_gather(own_gates, (WX, WC), axis=0, tiled=True)
    cot = flat(cotangent)
    cot_all = lax.all_gather(cot, SZ)
    cot_core = swap(cot, WC)
    source = wide(flat(inputs))
    norm_scale = lax.rsqrt(jnp.mean(source * source, axis=-1, keepdims=True) + 1e-06)
    normed = low(source * norm_scale * gain)
    keep, send = split_columns(normed, wx, wc)
    line.mark(send)
    recv = swap(send, WX)
    normed_turned = line.mark(line(normed)[0].T)

    sent, own_x = project(*line(recv, keep, w_x, oth_x))
    line.mark(sent)
    recv_x = swap(sent, WX)
    sent, own_y = project(*line(recv, keep, w_y, oth_y))
    line.mark(sent)
    recv_y, cot_x = swap(after(sent, recv_x), WX), swap(after(cot, recv_x), WX)
    own_x, recv_x, own_y, recv_y = cube(own_x), cube(recv_x), cube(own_y), cube(recv_y)
    tail_own, tail_recv = line(own_x[:, edge:], recv_x[:, edge:])
    tail = along_seq(line.mark(low(tail_own + wide(tail_recv))), 1)
    own_x, recv_x, tail, gates = line(own_x, recv_x, tail, gates)
    halo = jnp.pad(wide(tail), ((0, 0), (HALO - (taps - 1), 0), (0, 0)))
    branch_x, conv, gate_rec, gate_in, running, local_state, ends = recur(
        own_x,
        recv_x,
        halo,
        places,
        conv_w,
        as_row(conv_b),
        gates,
        as_row(bias_a),
        as_row(bias_i),
        as_row(decay_log),
    )
    line.mark(ends)
    other_ends = swap(ends, SY)
    ends, other_ends = line(ends, other_ends)
    joined = line.mark(carry_join(ends, other_ends, sy, 1))
    arrived = carry_shifts(joined, 1)
    own_y, recv_y = line(own_y, recv_y)
    branch_y = line.mark(gelu_pair(own_y + wide(recv_y))[0])
    carry = carry_finish(*tied_carry(line, other_ends, arrived), sy, 1)
    mixed = flat(low((local_state + running * carry) * branch_y))
    keep, send = split_columns(mixed, wx, wc)
    line.mark(send)
    recv = swap(send, WX)
    cot_x, mixed = line(cot_x, mixed)
    cot_both = swap(cot_x, WC)
    cot_x_far = [None if 2 * j == far else around(cot_x, j) for j in range(1, far)]
    both_turned = line.mark(jnp.concatenate([normed_turned, mixed.T], axis=1))
    recv, keep, oth_out, cot_all = line(recv, keep, oth_out, cot_all)
    sent, own = project(recv, keep, w_out, oth_out)
    line.mark(sent)
    recv = swap(sent, WX)
    pulled_units = line.mark(pull_units(line(cot, cot_core, cot_x, cot_both), w_down))
    own, recv = line(own, recv)
    stream = source + own + wide(recv)
    second_scale = lax.rsqrt(jnp.mean(stream * stream, axis=-1, keepdims=True) + 1e-06)
    normed_two = line.mark(low(stream * second_scale * gain2))

    normed_x, normed_core = swap(normed_two, WX), swap(normed_two, WC)
    normed_all = lax.all_gather(normed_two, SZ)
    core_of = lambda values: [swap(v, WC) for v in values]
    turned = both_turned.reshape(far, 2, 2, 2, features // (8 * far), half)
    turned, cot_x_far = line_tree(line, turned, cot_x_far)
    mine_x, send_x = rows_for(WX, 2, turned)
    got_x = swap(line.mark(send_x), WX)
    normed_both = swap(normed_x, WC)
    opposite = lambda v: lax.dynamic_index_in_dim(v, (sz + far // 2) % far, 0, keepdims=False)
    across = lambda pieces, gathered: [
        swap(opposite(gathered), WX) if v is None else v for v in pieces
    ]
    tied = line(normed_two, normed_core, normed_x, normed_both)
    normed_x_far = [None if 2 * j == far else around(tied[2], j) for j in range(1, far)]
    cot_x_far = across(cot_x_far, after(cot_all, tied[2]))
    acted = units(tied, w_gate, w_up, pulled_units)
    hidden, gate_grad, up_grad = acted
    line.mark(hidden)
    mine_y, send_y = rows_for(SY, 2, jnp.stack(line(mine_x, got_x)))
    got_y = swap(line.mark(send_y), SY)
    pulled = line.mark(units_back(*line(gate_grad, up_grad), w_gate, w_up))
    pulled_both, pulled_core = swap(pulled[half + rows :], WC), swap(pulled[rows:half], WC)
    pulled_there, pulled_both, got_y, normed_all, cot_x_far = line_tree(
        line, pulled[half : half + rows], pulled_both, got_y, normed_all, cot_x_far
    )
    for_x = line.mark(low(wide(pulled_there) + wide(pulled_both)))
    from_x = swap(for_x, WX)
    made = line.mark(units_made(*line(hidden), w_down))
    mine_y, got_y = line(mine_y, got_y)
    near, send = rows_for(WC, 2, jnp.concatenate([mine_y, got_y], axis=0))
    near, send = (v.reshape(4, features // 8, half) for v in (near, send))
    away = swap(line.mark(send), WC)
    pulled_here, pulled_core, from_x, normed_x_far = line_tree(
        line, pulled[:rows], pulled_core, from_x, normed_x_far
    )
    grad_normed_two = wide(pulled_here) + wide(pulled_core) + wide(from_x)
    weighted_two = grad_normed_two * gain2
    grad_stream = (
        wide(cot)
        + weighted_two * second_scale
        - stream * second_scale**3 * jnp.mean(weighted_two * stream, axis=-1, keepdims=True)
    )
    grad_gain2 = jnp.sum(grad_normed_two * stream * second_scale, axis=0)
    grad_proj = line.mark(low(grad_stream))
    proj_x, proj_y = swap(grad_proj, WX), swap(grad_proj, SY)
    normed_x_far = across(normed_x_far, normed_all)
    tied = line(cot_all, *cot_x_far)
    pull_here = line.mark(pull_of(spots, tied[0], tied[1:], w_down))

    cot_core_all, cot_both_far = swap(cot_all, WC), core_of(cot_x_far)
    normed_core_all = swap(normed_all, WC)
    cot_here, cot_there = (cot_all, cot_x_far), (cot_core_all, cot_both_far)

    def shared(gathered, pieces, pulled):
        gathered, pulled, *pieces = line(gathered, pulled, *pieces)
        acts = share_of(spots, gathered, pieces, w_gate, w_up, pulled)
        line.mark(acts[0])
        return acts

    def unit_sums(here, there, own_x, kinds):
        acts = [line(acted[k], acts_here[k], acts_there[k]) for k in kinds]
        outs = grad_of(spots, here, there, line(*own_x), acts)
        line.mark(outs[0])
        return [(outs[2 * i], swap(outs[2 * i + 1], SY)) for i in range(len(kinds))]

    def unit_join(mine, got):
        mine, got = line(mine, got)
        both = low(mine + wide(got))
        own, other = pick(parity, both[0], both[1]), pick(parity, both[1], both[0])
        line.mark(other)
        return own, partner_far(other)

    window, offset = window_of(held)

    def unit_final(own, other):
        own, other = line(own, other)
        parts = pick(parity, own, other), pick(parity, other, own)
        return wide(jnp.concatenate([parts[0], parts[1][:, window - offset :]], axis=1))

    def token_grad_of(second, *pieces):
        pieces = [*pieces, *core_of(pieces)]
        return line.mark(token_grad(*line(near, away), second, line(*pieces)))

    proj_x, proj_y, grad_proj = line(proj_x, proj_y, grad_proj)
    sent, own = project_back([(proj_x, grad_proj, w_out, oth_out)])
    line.mark(sent)
    sent, proj_xy = swap(sent, WX), swap(proj_x, SY)
    tied = line(cot_core_all, *cot_both_far)
    pull_there = line.mark(pull_of(spots, tied[0], tied[1:], w_down))
    sent, own, proj_xy, normed_x_far = line_tree(line, sent, own, proj_xy, normed_x_far)
    normed_both_far = core_of(normed_x_far)
    normed_here, normed_there = (normed_all, normed_x_far), (normed_core_all, normed_both_far)
    grad_mixed = cube(join_columns(own, wide(sent), wx, wc))
    line.mark(grad_mixed)
    grad_pre, behind, local_grad, back_ends = unroll(
        *line(grad_mixed, own_y, recv_y, running, local_state, carry, gate_rec),
        places,
        as_row(decay_log),
        head,
    )
    line.mark(back_ends)
    grad_pre = flat(grad_pre)
    other_ends = swap(back_ends, SY)
    pre_x, pre_y = swap(grad_pre, WX), swap(grad_pre, SY)
    back_ends, other_ends = line(back_ends, other_ends)
    joined = line.mark(carry_join(back_ends, other_ends, sy, -1))
    arrived = carry_shifts(joined, -1)
    acts_here = shared(*normed_here, pull_here)
    other_ends, pre_x, pre_y, *arrived = line(other_ends, pre_x, pre_y, *arrived)
    carry_back = carry_finish(other_ends, arrived, sy, -1)
    line.mark(carry_back)
    spread, earlier, grad_wa, grad_wi, sums = recur_back(
        *line(behind, local_grad, carry_back, running, local_state, carry),
        gate_rec,
        gate_in,
        conv,
        branch_x,
        halo,
        places,
        conv_w,
        gates,
        as_row(decay_log),
    )
    line.mark(earlier)
    pre_xy = swap(pre_x, SY)
    later = along_seq(low(earlier[:, HALO - (taps - 1) :]), -1)
    out_sums = scatter_far(token_grad_of(1, grad_proj, proj_x, proj_y, proj_xy))
    grad_wa, grad_wi, sums, grad_gain2 = line(grad_wa, grad_wi, sums, grad_gain2)
    small = jnp.concatenate([grad_gain2[None], sums], axis=0)
    small = low(jnp.pad(small.T, ((0, 0), (0, 128 - small.shape[0]))))
    rest = jnp.concatenate([grad_wa, grad_wi, small], axis=1)
    rest = line.mark(rest).reshape(far, 2, 2, 2, features // (8 * far), -1)

    def rest_step(axis, place, value):
        mine, send = rows_for(axis, place, value)
        line.mark(send)
        return mine, swap(send, axis)

    def rest_join(mine, got):
        mine, got = line(mine, got)
        return low(wide(mine) + wide(got))

    rest = rest_step(WC, 3, rest)
    spread, later = line(spread, later)
    grad_branch = flat(low(spread + jnp.pad(wide(later), ((0, 0), (edge, 0), (0, 0)))))
    line.mark(grad_branch)
    branch_x_part, branch_y_part = swap(grad_branch, WX), swap(grad_branch, SY)
    rest = rest_step(WX, 2, rest_join(*rest))
    acts_there = shared(*normed_there, pull_there)
    branch_x_part, branch_y_part, pre_xy = line(branch_x_part, branch_y_part, pre_xy)
    sent, own = project_back(
        [
            line(branch_x_part, grad_branch, w_x, oth_x),
            line(pre_x, grad_pre, w_y, oth_y),
        ]
    )
    line.mark(sent)
    sent = swap(sent, WX)
    branch_xy_part = swap(branch_y_part, WX)
    (down,) = unit_sums(cot_here, cot_there, (cot_x, cot_both), [0])
    rest = rest_step(SY, 1, rest_join(*rest))
    sent, own, branch_xy_part, out_sums = line(sent, own, branch_xy_part, out_sums)
    grad_normed = join_columns(own, wide(sent), wx, wc)
    weighted = grad_normed * gain
    input_grad = (
        grad_stream
        + weighted * norm_scale
        - source * norm_scale**3 * jnp.mean(weighted * source, axis=-1, keepdims=True)
    )
    grad_gain = jnp.sum(grad_normed * source * norm_scale, axis=0)
    line.mark(grad_gain)

    y_sums = scatter_far(token_grad_of(0, grad_pre, pre_x, pre_y, pre_xy))
    (gate,) = unit_sums(normed_here, normed_there, (normed_x, normed_both), [1])
    x_grad = token_grad_of(0, grad_branch, branch_x_part, branch_y_part, branch_xy_part)

    down = unit_join(*down)
    (up,) = unit_sums(normed_here, normed_there, (normed_x, normed_both), [2])
    rest = rest_join(*rest).reshape(features // 8, -1)
    late_sums = scatter_far(line.mark(jnp.concatenate([x_grad, rest], axis=1)))
    gate = unit_join(*gate)
    (y_sums,) = line(y_sums)
    up = unit_join(*up)
    grad_gain = total_of_all(*line(grad_gain))
    made_there, made_both = line(made[half : half + rows], swap(after(made, grad_mixed)[half + rows :], WC))
    made_x = swap(line.mark(low(wide(made_there) + wide(made_both))), WX)
    made_core = swap(after(made, grad_mixed)[rows:half], WC)
    down_grad = line.mark(unit_final(*down).T)
    made_here, made_core, made_x = line(made[:rows], made_core, made_x)
    output = line.mark(low(stream + wide(made_here) + wide(made_core) + wide(made_x)))
    gate_grad = line.mark(unit_final(*gate))
    up_grad = line.mark(unit_final(*up))
    x_sums, rest = late_sums[:, :features], wide(late_sums[:, features:])
    grads = rest[:, 2 * head :]
    return (
        cube(output),
        cube(input_grad),
        grad_gain,
        wide(x_sums),
        wide(y_sums),
        grads[:, 1 : 1 + taps].T,
        grads[:, 1 + taps],
        rest[:, :head],
        grads[:, 2 + taps],
        rest[:, head : 2 * head],
        grads[:, 3 + taps],
        grads[:, 4 + taps],
        wide(out_sums),
        grads[:, 0],
        gate_grad,
        up_grad,
        down_grad,
    )


def solution(mesh):
    seq, wt = mesh.devices.shape
    split = Mesh(mesh.devices.reshape(seq // 2, 2, wt // 2, 2), (SZ, SY, WX, WC))
    s, w = (SZ, SY), (WX, WC)
    everywhere = (SZ, SY, WX, WC)
    return jax.shard_map(
        local,
        mesh=split,
        in_specs=(
            P(w, s, None),
            P(w, s),
            P(w, s, None),
            P(),
            P(w, None),
            P(w, None),
            P(),
            P(),
            P(w, None),
            P(),
            P(w, None),
            P(),
            P(),
            P(w, None),
            P(),
            P(None, w),
            P(None, w),
            P(w, None),
        ),
        out_specs=(
            P(w, s, None),
            P(w, s, None),
            P(everywhere),
            P(everywhere, None),
            P(everywhere, None),
            P(None, everywhere),
            P(everywhere),
            P(everywhere, None),
            P(everywhere),
            P(everywhere, None),
            P(everywhere),
            P(everywhere),
            P(everywhere, None),
            P(everywhere),
            P(s, w),
            P(s, w),
            P(w, s),
        ),
        check_vma=False,
    )
```

```python
from functools import partial

import jax
import jax.numpy as jnp
from jax import lax
from jax.experimental import pallas as pl
from jax.experimental.pallas import tpu as pltpu
from jax.sharding import Mesh
from jax.sharding import PartitionSpec as P

SZ, SY, WX, WC = ("sz", "sy", "wx", "wc")
F32, BF16 = (jnp.float32, jnp.bfloat16)
HALO = 8
ROOT_2_PI = 0.7978845608028654
CUBIC = 0.044715
VMEM_GRANT = 58 << 20
COST_SHARE = 0.02
HEADS_EACH = 2


def swap(value, axis):
    return lax.ppermute(value, axis, [(0, 1), (1, 0)])


def shift(value, axis, steps):
    count = lax.axis_size(axis)
    initial, last = (max(0, -steps), min(count, count - steps))
    return lax.ppermute(value, axis, [(source, source + steps) for source in range(initial, last)])


def around(value, steps):
    count = lax.axis_size(SZ)
    return lax.ppermute(value, SZ, [((to + steps) % count, to) for to in range(count)])


def partner_far(value):
    count = lax.axis_size(SZ)
    return lax.ppermute(value, SZ, [(source, source ^ 1) for source in range(count)])


def along_seq(value, steps):
    count = lax.axis_size(SZ) * lax.axis_size(SY)
    initial, last = (max(0, -steps), min(count, count - steps))
    return lax.ppermute(
        value, (SZ, SY), [(source, source + steps) for source in range(initial, last)]
    )


def pick(bit, zero, one):
    return jnp.where(bit == 0, zero, one)


def after(value, *others):
    return lax.optimization_barrier((value, *others))[0]


def tie(*values):
    return lax.optimization_barrier(values)


class Line:
    def __init__(self):
        self.last = None
        self.held = []

    def __call__(self, *values):
        others = self.held + ([] if self.last is None else [self.last])
        self.held = []
        return lax.optimization_barrier((*values, *others))[: len(values)]

    def hold(self, *values):
        self.held += values

    def mark(self, value):
        self.last = value
        return value


def gelu_pair(value):
    square = value * value
    tanh = jnp.tanh(ROOT_2_PI * value * (1.0 + CUBIC * square))
    half = 0.5 * (1.0 + tanh)
    slope = half + 0.5 * value * (1.0 - tanh * tanh) * (
        ROOT_2_PI * (1.0 + 3.0 * CUBIC * square)
    )
    return value * half, slope


def dot(left, right):
    return jnp.dot(left, right, preferred_element_type=F32)


def dot_nt(left, right):
    return lax.dot_general(left, right, (((1,), (1,)), ((), ())), preferred_element_type=F32)


def dot_tn(left, right):
    return lax.dot_general(left, right, (((0,), (0,)), ((), ())), preferred_element_type=F32)


def params():
    return pltpu.CompilerParams(
        dimension_semantics=("arbitrary",), vmem_limit_bytes=VMEM_GRANT
    )


def cost(flops, nbytes):
    return pl.CostEstimate(
        flops=int(flops * COST_SHARE), bytes_accessed=int(nbytes * COST_SHARE), transcendentals=0
    )


def split_columns(value, wx, wc):
    quarter = value.shape[-1] // 4
    parts = [value[..., i * quarter : (i + 1) * quarter] for i in range(4)]
    near = [pick(wx, parts[0], parts[2]), pick(wx, parts[1], parts[3])]
    far = [pick(wx, parts[2], parts[0]), pick(wx, parts[3], parts[1])]
    keep = jnp.concatenate([pick(wc, near[0], near[1]), pick(wc, near[1], near[0])], axis=-1)
    send = jnp.concatenate([pick(wc, far[0], far[1]), pick(wc, far[1], far[0])], axis=-1)
    return keep, send


def join_columns(near, far, wx, wc):
    near = [pick(wc, near[0], near[1]), pick(wc, near[1], near[0])]
    far = [pick(wc, far[0], far[1]), pick(wc, far[1], far[0])]
    return jnp.concatenate(
        [
            pick(wx, near[0], far[0]),
            pick(wx, near[1], far[1]),
            pick(wx, far[0], near[0]),
            pick(wx, far[1], near[1]),
        ],
        axis=-1,
    )


def project(recv, keep, weight):
    rows = recv.shape[0]
    total = dot(jnp.concatenate([recv, keep], axis=0), weight)
    return total[:rows].astype(BF16), total[rows:]


def project_back(terms):
    rows = terms[0][0].shape[0]
    total = 0.0
    for recv, own, weight in terms:
        total = total + dot_nt(jnp.concatenate([recv, own], axis=0), weight)
    half = total.shape[1] // 2
    total = jnp.stack([total[:, :half], total[:, half:]])
    return total[:, :rows].astype(BF16), total[:, rows:]


def less_one_exp(value):
    series = 1.0
    for n in (9, 8, 7, 6, 5, 4, 3, 2):
        series = 1.0 + value * (1.0 / n) * series
    return jnp.where(value > -0.5, -value * series, 1.0 - jnp.exp(value))


def shifted_down(value, steps, fill):
    edge = jnp.full((value.shape[0], steps, value.shape[2]), fill, F32)
    return jnp.concatenate([edge, value[:, : value.shape[1] - steps]], axis=1)


def shifted_up(value, steps, fill):
    edge = jnp.full((value.shape[0], steps, value.shape[2]), fill, F32)
    return jnp.concatenate([value[:, steps:], edge], axis=1)


def scan_rows(decay, driven, mover):
    steps = 1
    while steps < decay.shape[1]:
        driven = driven + decay * mover(driven, steps, 0.0)
        decay = decay * mover(decay, steps, 1.0)
        steps *= 2
    return decay, driven


def tap_mask(places, offset):
    return (places >= offset).astype(F32)


def by_head(flat, gate, product):
    head = gate.shape[1]
    spans = [slice(i, i + head) for i in range(0, flat.shape[1], head)]
    return jnp.concatenate([product(flat[:, s], gate[s]) for s in spans], axis=1)


def recur_kernel(
    own,
    recv,
    halo,
    places,
    conv_w,
    conv_b,
    gate_a,
    gate_i,
    bias_a,
    bias_i,
    decay_log,
    branch_out,
    conv_out,
    rec_out,
    in_out,
    run_out,
    state_out,
    ends_out,
):
    batches, length, width = own.shape
    branch = (own[...] + recv[...].astype(F32)).astype(BF16)
    branch_out[...] = branch
    extended = jnp.concatenate([halo[...], branch.astype(F32)], axis=1)
    spot = places[...]
    total = jnp.zeros((batches, length, width), F32) + conv_b[...][None]
    for offset in range(conv_w.shape[0]):
        moved = extended[:, HALO - offset : HALO - offset + length]
        total = total + conv_w[offset : offset + 1][None] * moved * tap_mask(spot, offset)
    conv = total.astype(BF16)
    conv_out[...] = conv
    flat = conv.reshape(batches * length, width)
    shape = (batches, length, width)
    gate_rec = jax.nn.sigmoid(by_head(flat, gate_a, dot) + bias_a[...]).reshape(shape)
    gate_in = jax.nn.sigmoid(by_head(flat, gate_i, dot) + bias_i[...]).reshape(shape)
    rec_out[...] = gate_rec
    in_out[...] = gate_in
    log_a = -8.0 * gate_rec * jnp.exp(decay_log[...])[None]
    alive = tap_mask(spot, 1)
    root = jnp.sqrt(less_one_exp(2.0 * log_a))
    multiplier = alive * root + (1.0 - alive)
    decay = jnp.exp(log_a) * alive
    driven = conv.astype(F32) * gate_in * multiplier
    running, state = scan_rows(decay, driven, shifted_down)
    run_out[...] = running
    state_out[...] = state
    for b in range(batches):
        ends_out[b : b + 1] = running[b, length - 1 :]
        ends_out[batches + b : batches + b + 1] = state[b, length - 1 :]


def head_specs(batches, length, head, taps, group=1):
    head = head * group
    tokens = pl.BlockSpec((batches, length, head), lambda h: (0, 0, h))
    edge = pl.BlockSpec((batches, HALO, head), lambda h: (0, 0, h))
    place = pl.BlockSpec((batches, length, 1), lambda h: (0, 0, 0))
    row = pl.BlockSpec((1, head), lambda h: (0, h))
    tap = pl.BlockSpec((taps, head), lambda h: (0, h))
    gates = [
        pl.BlockSpec((head, head // group), lambda h: (h, 0)),
        pl.BlockSpec((head, head // group), lambda h: (h, 1)),
    ]
    ends = pl.BlockSpec((2 * batches, head), lambda h: (0, h))
    carry = pl.BlockSpec((batches, 1, head), lambda h: (0, 0, h))
    return tokens, edge, place, row, tap, gates, ends, carry


def recur(own, recv, halo, places, conv_w, conv_b, gates, bias_a, bias_i, decay_log):
    batches, length, features = own.shape
    head = gates.shape[1] // 2
    tokens, edge, place, row, tap, gate, ends, _ = head_specs(
        batches, length, head, conv_w.shape[0], HEADS_EACH
    )
    full = lambda dtype: jax.ShapeDtypeStruct((batches, length, features), dtype)
    return pl.pallas_call(
        recur_kernel,
        grid=(features // (head * HEADS_EACH),),
        in_specs=[tokens, tokens, edge, place, tap, row, *gate, row, row, row],
        out_specs=[tokens] * 6 + [ends],
        out_shape=[full(BF16), full(BF16)]
        + [full(F32)] * 4
        + [jax.ShapeDtypeStruct((2 * batches, features), F32)],
        compiler_params=params(),
        cost_estimate=cost(200 * batches * length * features, 40 * batches * length * features),
        name="recur",
    )(own, recv, halo, places, conv_w, conv_b, gates, gates, bias_a, bias_i, decay_log)


def unroll_kernel(
    mixed_grad,
    own_y,
    recv_y,
    running,
    local_state,
    carry,
    gate_rec,
    places,
    decay_log,
    pre_out,
    behind_out,
    local_out,
    ends_out,
):
    batches, length, _ = mixed_grad.shape
    pulled = mixed_grad[...].astype(F32)
    branch_y, slope = gelu_pair(own_y[...] + recv_y[...].astype(F32))
    state = local_state[...] + running[...] * carry[...]
    pre_out[...] = (pulled * state * slope).astype(BF16)
    log_a = -8.0 * gate_rec[...] * jnp.exp(decay_log[...])[None]
    decay = jnp.exp(log_a) * tap_mask(places[...], 1)
    following = shifted_up(decay, 1, 1.0)
    behind, local = scan_rows(following, pulled * branch_y, shifted_up)
    behind_out[...] = behind
    local_out[...] = local
    for b in range(batches):
        ends_out[b : b + 1] = running[b, length - 1 :, :]
        ends_out[batches + b : batches + b + 1] = decay[b, :1] * local[b, :1]


def unroll(mixed_grad, own_y, recv_y, running, local_state, carry, gate_rec, places, decay_log, head):
    batches, length, features = mixed_grad.shape
    tokens, _, place, row, _, _, ends, carried = head_specs(batches, length, head, 1, HEADS_EACH)
    full = lambda dtype: jax.ShapeDtypeStruct((batches, length, features), dtype)
    return pl.pallas_call(
        unroll_kernel,
        grid=(features // (head * HEADS_EACH),),
        in_specs=[tokens] * 5 + [carried, tokens, place, row],
        out_specs=[tokens] * 3 + [ends],
        out_shape=[full(BF16), full(F32), full(F32)]
        + [jax.ShapeDtypeStruct((2 * batches, features), F32)],
        compiler_params=params(),
        cost_estimate=cost(200 * batches * length * features, 40 * batches * length * features),
        name="unroll",
    )(mixed_grad, own_y, recv_y, running, local_state, carry, gate_rec, places, decay_log)


def recur_back_kernel(
    behind,
    local_grad,
    carry_back,
    running,
    local_state,
    carry,
    gate_rec,
    gate_in,
    conv,
    branch,
    halo,
    places,
    conv_w,
    gate_a,
    gate_i,
    decay_log,
    spread_out,
    earlier_out,
    wa_out,
    wi_out,
    sums_out,
):
    batches, length, width = behind.shape
    shape = (batches, length, width)
    rows = batches * length
    spot = places[...]
    alive = tap_mask(spot, 1)
    rate = jnp.exp(decay_log[...])[None]
    rec, inner = gate_rec[...], gate_in[...]
    log_a = -8.0 * rec * rate
    raw = jnp.exp(log_a)
    root = jnp.sqrt(less_one_exp(2.0 * log_a))
    multiplier = alive * root + (1.0 - alive)
    conv_low = conv[...]
    conv_full = conv_low.astype(F32)
    grad_state = local_grad[...] + behind[...] * carry_back[...]
    state = local_state[...] + running[...] * carry[...]
    before = jnp.concatenate([carry[...], state[:, : length - 1]], axis=1)
    scaled = grad_state * conv_full * inner
    grad_log = alive * raw * (grad_state * before - scaled * raw / root)
    grad_a = grad_log * (-8.0 * rate) * rec * (1.0 - rec)
    grad_i = scaled * multiplier * (1.0 - inner)
    low_a = grad_a.astype(BF16).reshape(rows, width)
    low_i = grad_i.astype(BF16).reshape(rows, width)
    pulled = grad_state * inner * multiplier
    pulled = pulled + (
        by_head(low_a, gate_a, dot_nt) + by_head(low_i, gate_i, dot_nt)
    ).reshape(shape)
    pulled = pulled.astype(BF16).astype(F32)
    flat = conv_low.reshape(rows, width)
    head = gate_a.shape[1]
    for i in range(0, width, head):
        span = slice(i, i + head)
        wa_out[span] = dot_tn(flat[:, span], low_a[:, span]).astype(BF16)
        wi_out[span] = dot_tn(flat[:, span], low_i[:, span]).astype(BF16)
    extended = jnp.concatenate([halo[...], branch[...].astype(F32)], axis=1)
    taps = conv_w.shape[0]
    spread = jnp.zeros((batches, length + HALO, width), F32)
    blank = jnp.zeros((batches, HALO, width), F32)
    sums = []
    add = lambda value: jnp.sum(value.reshape(rows, width), axis=0, keepdims=True)
    for offset in range(taps):
        masked = pulled * tap_mask(spot, offset)
        weighted = jnp.concatenate([blank, conv_w[offset : offset + 1][None] * masked], axis=1)
        spread = spread + (shifted_up(weighted, offset, 0.0) if offset else weighted)
        sums.append(add(masked * extended[:, HALO - offset : HALO - offset + length]))
    earlier_out[...] = spread[:, :HALO]
    spread_out[...] = spread[:, HALO:]
    sums += [add(pulled), add(grad_a), add(grad_i), add(grad_log * log_a)]
    sums_out[...] = jnp.concatenate(sums, axis=0)


def recur_back(
    behind,
    local_grad,
    carry_back,
    running,
    local_state,
    carry,
    gate_rec,
    gate_in,
    conv,
    branch,
    halo,
    places,
    conv_w,
    gates,
    decay_log,
):
    batches, length, features = behind.shape
    head = gates.shape[1] // 2
    taps = conv_w.shape[0]
    tokens, edge, place, row, tap, gate, _, carried = head_specs(
        batches, length, head, taps, HEADS_EACH
    )
    block = pl.BlockSpec((head * HEADS_EACH, head), lambda h: (h, 0))
    return pl.pallas_call(
        recur_back_kernel,
        grid=(features // (head * HEADS_EACH),),
        in_specs=[tokens, tokens, carried, tokens, tokens, carried]
        + [tokens] * 4
        + [edge, place, tap, *gate, row],
        out_specs=[
            tokens,
            edge,
            block,
            block,
            pl.BlockSpec((taps + 4, head * HEADS_EACH), lambda h: (0, h)),
        ],
        out_shape=[
            jax.ShapeDtypeStruct((batches, length, features), F32),
            jax.ShapeDtypeStruct((batches, HALO, features), F32),
            jax.ShapeDtypeStruct((features, head), BF16),
            jax.ShapeDtypeStruct((features, head), BF16),
            jax.ShapeDtypeStruct((taps + 4, features), F32),
        ],
        compiler_params=params(),
        cost_estimate=cost(300 * batches * length * features, 50 * batches * length * features),
        name="recur_back",
    )(
        behind,
        local_grad,
        carry_back,
        running,
        local_state,
        carry,
        gate_rec,
        gate_in,
        conv,
        branch,
        halo,
        places,
        conv_w,
        gates,
        gates,
        decay_log,
    )


def unit_step(gate_pre, up_pre, pulled, hidden_out, gate_out, up_out):
    act, slope = gelu_pair(gate_pre)
    hidden_out[...] = (act * up_pre).astype(BF16)
    gate_out[...] = (pulled * up_pre * slope).astype(BF16)
    up_out[...] = (pulled * act).astype(BF16)


def fill(target, pieces):
    start = 0
    for piece in pieces:
        target[start : start + piece.shape[0]] = piece
        start += piece.shape[0]


def units_kernel(count, *refs):
    pieces, (w_gate, w_up, pulled, hidden_out, gate_out, up_out, tokens) = refs[:count], refs[count:]

    @pl.when(pl.program_id(0) == 0)
    def _():
        fill(tokens, [p[...] for p in pieces])

    gate_pre, up_pre = dot(tokens[...], w_gate[...]), dot(tokens[...], w_up[...])
    unit_step(gate_pre, up_pre, pulled[...].astype(F32), hidden_out, gate_out, up_out)


def units(pieces, w_gate, w_up, pulled):
    count = len(pieces)
    rows, width = pieces[0].shape
    held = w_gate.shape[1]
    tile = 640
    whole = pl.BlockSpec((rows, width), lambda j: (0, 0), pipeline_mode=pl.Buffered(1))
    column = pl.BlockSpec((width, tile), lambda j: (0, j))
    out = pl.BlockSpec((count * rows, tile), lambda j: (0, j))
    return pl.pallas_call(
        partial(units_kernel, count),
        grid=(held // tile,),
        in_specs=[whole] * count + [column, column, out],
        out_specs=[out] * 3,
        out_shape=[jax.ShapeDtypeStruct((count * rows, held), BF16)] * 3,
        scratch_shapes=[pltpu.VMEM((count * rows, width), BF16)],
        compiler_params=params(),
        cost_estimate=cost(4 * count * rows * width * held, 4 * width * held),
        name="units",
    )(*pieces, w_gate, w_up, pulled)


def pull_units_kernel(count, *refs):
    pieces, (w_down, out, tokens) = refs[:count], refs[count:]

    @pl.when(pl.program_id(0) == 0)
    def _():
        fill(tokens, [p[...] for p in pieces])

    out[...] = dot_nt(tokens[...], w_down[...]).astype(BF16)


def pull_units(pieces, w_down):
    count = len(pieces)
    rows, width = pieces[0].shape
    held = w_down.shape[0]
    tile = 640
    whole = pl.BlockSpec((rows, width), lambda j: (0, 0), pipeline_mode=pl.Buffered(1))
    return pl.pallas_call(
        partial(pull_units_kernel, count),
        grid=(held // tile,),
        in_specs=[whole] * count + [pl.BlockSpec((tile, width), lambda j: (j, 0))],
        out_specs=pl.BlockSpec((count * rows, tile), lambda j: (0, j)),
        out_shape=jax.ShapeDtypeStruct((count * rows, held), BF16),
        scratch_shapes=[pltpu.VMEM((count * rows, width), BF16)],
        compiler_params=params(),
        cost_estimate=cost(2 * count * rows * width * held, 2 * width * held),
        name="pull_units",
    )(*pieces, w_down)


def spill(total, outs):
    rows = outs[0].shape[0]
    for i, out in enumerate(outs):
        out[...] = total[i * rows : (i + 1) * rows].astype(BF16)


def units_back_kernel(gate, up, w_gate, w_up, *outs):
    spill(dot_nt(gate[...], w_gate[...]) + dot_nt(up[...], w_up[...]), outs)


def units_back(gate, up, w_gate, w_up):
    tile = 640
    rows = gate.shape[0]
    width, held = w_gate.shape
    whole = pl.BlockSpec((rows, held), lambda j: (0, 0), pipeline_mode=pl.Buffered(1))
    row = pl.BlockSpec((tile, held), lambda j: (j, 0))
    return pl.pallas_call(
        units_back_kernel,
        grid=(width // tile,),
        in_specs=[whole, whole, row, row],
        out_specs=[pl.BlockSpec((rows // 4, tile), lambda j: (0, j))] * 4,
        out_shape=[jax.ShapeDtypeStruct((rows // 4, width), BF16)] * 4,
        compiler_params=params(),
        cost_estimate=cost(4 * rows * width * held, 4 * width * held),
        name="units_back",
    )(gate, up, w_gate, w_up)


def units_made_kernel(hidden, w_down, *outs):
    spill(dot(hidden[...], w_down[...]), outs)


def units_made(hidden, w_down):
    tile = 1280
    rows, held = hidden.shape
    width = w_down.shape[1]
    return pl.pallas_call(
        units_made_kernel,
        grid=(width // tile,),
        in_specs=[
            pl.BlockSpec((rows, held), lambda j: (0, 0), pipeline_mode=pl.Buffered(1)),
            pl.BlockSpec((held, tile), lambda j: (0, j)),
        ],
        out_specs=[pl.BlockSpec((rows // 4, tile), lambda j: (0, j))] * 4,
        out_shape=[jax.ShapeDtypeStruct((rows // 4, width), BF16)] * 4,
        compiler_params=params(),
        cost_estimate=cost(2 * rows * width * held, 2 * width * held),
        name="units_made",
    )(hidden, w_down)


def window_of(held):
    width = -(-held // 2 // 128) * 128
    return width, held - width


def at_distance(places, gathered, steps):
    count = gathered[0].shape[0]
    return [gathered[0][(places[0] + steps) % count], *[part[steps] for part in gathered[1:]]]


def others(places, gathered):
    count = gathered[0].shape[0]
    return [v for steps in range(1, count) for v in at_distance(places, gathered, steps)]


def share_pull_kernel(count, places, *refs):
    gathered, (w_down, out, tokens) = refs[:count], refs[count:]

    @pl.when(pl.program_id(0) == 0)
    def _():
        fill(tokens, others(places, gathered))

    out[...] = dot_nt(tokens[...], w_down[...]).astype(BF16)


def share_kernel(count, places, *refs):
    gathered, refs = refs[:count], refs[count:]
    w_gate, w_up, pulled, hidden_out, gate_out, up_out, tokens = refs

    @pl.when(pl.program_id(0) == 0)
    def _():
        fill(tokens, others(places, gathered))

    gate_pre, up_pre = dot(tokens[...], w_gate[...]), dot(tokens[...], w_up[...])
    unit_step(gate_pre, up_pre, pulled[...].astype(F32), hidden_out, gate_out, up_out)


def share_call(kernel, places, gathered, weights, more, outs, name):
    count, rows, width = gathered[0].shape
    tile = 512
    held = weights[0].shape[0] if weights[0].shape[1] == width else weights[0].shape[1]
    window, offset = window_of(held)
    total = len(gathered) * (count - 1) * rows
    specs = []
    for weight in weights:
        if weight.shape[1] == width:
            specs.append(
                pl.BlockSpec(
                    (pl.Element(tile), pl.Element(width)),
                    lambda j, places: (pl.multiple_of(places[1] * offset + j * tile, 128), 0),
                )
            )
        else:
            specs.append(
                pl.BlockSpec(
                    (pl.Element(width), pl.Element(tile)),
                    lambda j, places: (0, pl.multiple_of(places[1] * offset + j * tile, 128)),
                )
            )
    out = pl.BlockSpec((total, tile), lambda j, places: (0, j))
    whole = pl.BlockSpec(
        gathered[0].shape, lambda j, places: (0, 0, 0), pipeline_mode=pl.Buffered(1)
    )
    return pl.pallas_call(
        partial(kernel, len(gathered)),
        grid_spec=pltpu.PrefetchScalarGridSpec(
            num_scalar_prefetch=1,
            grid=(window // tile,),
            in_specs=[whole] * len(gathered) + specs + [out] * len(more),
            out_specs=[out] * outs,
            scratch_shapes=[pltpu.VMEM((total, width), BF16)],
        ),
        out_shape=[jax.ShapeDtypeStruct((total, window), BF16)] * outs,
        compiler_params=params(),
        cost_estimate=cost(
            2 * len(weights) * total * width * window, 2 * len(weights) * width * window
        ),
        name=name,
    )(places, *gathered, *weights, *more)


def share_pull(places, gathered, w_down):
    return share_call(share_pull_kernel, places, gathered, [w_down], [], 1, "share_pull")[0]


def share(places, gathered, w_gate, w_up, pulled):
    return share_call(share_kernel, places, gathered, [w_gate, w_up], [pulled], 3, "share")


def unit_grad_kernel(count, kinds, places, *refs):
    here, there, refs = refs[:count], refs[count : 2 * count], refs[2 * count :]
    acts, outs = refs[: 3 * kinds], refs[3 * kinds : 5 * kinds]
    left, whole = refs[5 * kinds :]
    block = whole.shape[0] // 2
    fill(
        left,
        at_distance(places, here, 0)
        + at_distance(places, there, 0)
        + others(places, here)
        + others(places, there),
    )
    own = pl.multiple_of(places[2] * block, block)
    other = pl.multiple_of((1 - places[2]) * block, block)
    for kind in range(kinds):
        parts = acts[3 * kind : 3 * kind + 3]
        total, start = None, 0
        for part in parts:
            size = part.shape[0]
            term = dot_tn(left[start : start + size], part[...])
            total = term if total is None else total + term
            start += size
        whole[...] = total
        outs[2 * kind][0] = whole[pl.ds(own, block)]
        outs[2 * kind + 1][0] = whole[pl.ds(other, block)].astype(BF16)


def unit_grad(places, here, there, acts):
    kinds = len(acts)
    count, rows, features = here[0].shape
    window, offset = window_of(acts[0][0].shape[1])
    width = features // count
    total = 2 * len(here) * count * rows
    once = pl.Buffered(1)
    gathered = pl.BlockSpec((count, rows, width), lambda i, p: (0, 0, 2 * (p[0] // 2) + i))
    mine = pl.BlockSpec(
        (pl.Element(2 * len(here) * rows), pl.Element(window)),
        lambda i, p: (0, pl.multiple_of(p[1] * offset, 128)),
        pipeline_mode=once,
    )
    act = pl.BlockSpec(acts[0][1].shape, lambda i, p: (0, 0), pipeline_mode=once)
    out = pl.BlockSpec((1, width // 2, window), lambda i, p: (i, 0, 0))
    shape = (2, width // 2, window)
    return pl.pallas_call(
        partial(unit_grad_kernel, len(here), kinds),
        grid_spec=pltpu.PrefetchScalarGridSpec(
            num_scalar_prefetch=1,
            grid=(2,),
            in_specs=[gathered] * (2 * len(here)) + [mine, act, act] * kinds,
            out_specs=[out] * (2 * kinds),
            scratch_shapes=[
                pltpu.VMEM((total, width), BF16),
                pltpu.VMEM((width, window), F32),
            ],
        ),
        out_shape=[jax.ShapeDtypeStruct(shape, d) for d in (F32, BF16)] * kinds,
        compiler_params=params(),
        cost_estimate=cost(4 * kinds * total * width * window, 2 * kinds * total * window),
        name="unit_grad",
    )(places, *here, *there, *[a for v in acts for a in v])


def window_part(value, places, axis):
    window, offset = window_of(value.shape[axis])
    return lax.dynamic_slice_in_dim(value, places[1] * offset, window, axis=axis)


def others_plain(places, gathered):
    features = gathered[0].shape[2]
    rolled = [jnp.roll(gathered[0], -places[0], axis=0), *gathered[1:]]
    return jnp.concatenate([v[1:] for v in rolled], axis=1).reshape(-1, features)


def share_pull_plain(places, gathered, w_down):
    tokens = others_plain(places, gathered)
    return dot_nt(tokens, window_part(w_down, places, 0)).astype(BF16)


def share_plain(places, gathered, w_gate, w_up, pulled):
    tokens = others_plain(places, gathered)
    act, slope = gelu_pair(dot(tokens, window_part(w_gate, places, 1)))
    up_pre = dot(tokens, window_part(w_up, places, 1))
    pulled = pulled.astype(F32)
    return [v.astype(BF16) for v in (act * up_pre, pulled * up_pre * slope, pulled * act)]


def unit_grad_plain(places, here, there, acts):
    count, _, features = here[0].shape
    block = features // (2 * count)
    at = lambda v: lax.dynamic_index_in_dim(v, places[0], 0, keepdims=False)
    own = [v for part in (here, there) for v in (at(part[0]), *[w[0] for w in part[1:]])]
    tokens = jnp.concatenate(
        own + [others_plain(places, here), others_plain(places, there)], axis=0
    )
    tokens = lax.dynamic_slice_in_dim(tokens, places[0] // 2 * 4 * block, 4 * block, axis=1)
    outs = []
    for own, *rest in acts:
        right = jnp.concatenate([window_part(own, places, 1), *rest], axis=0)
        whole = dot_tn(tokens, right).reshape(2, 2, block, -1)
        outs.append(pick(places[2], whole[:, 0], whole[:, 1]))
        outs.append(pick(places[2], whole[:, 1], whole[:, 0]).astype(BF16))
    return outs


def carry_join(ends, other, bit, direction):
    half = ends.shape[0] // 2
    is_last = bit if direction > 0 else 1 - bit
    first_end = pick(is_last, ends[half:], other[half:])
    last_end = pick(is_last, other[half:], ends[half:])
    last_run = pick(is_last, other[:half], ends[:half])
    return jnp.concatenate(
        [ends[:half] * other[:half], last_run * first_end + last_end], axis=0
    )


def carry_shifts(joined, direction):
    return [shift(joined, SZ, direction * k) for k in range(1, lax.axis_size(SZ))]


def line_tree(line, *values):
    leaves, tree = jax.tree.flatten(values)
    arrays = iter(line(*[v for v in leaves if not isinstance(v, int)]))
    return jax.tree.unflatten(tree, [v if isinstance(v, int) else next(arrays) for v in leaves])


def tied_carry(line, other, arrived):
    other, *arrived = line(other, *arrived)
    return other, arrived


def carry_finish(other, arrived, bit, direction):
    half = other.shape[0] // 2
    is_last = bit if direction > 0 else 1 - bit
    entering = jnp.zeros_like(other[half:])
    for far in reversed(arrived):
        entering = far[half:] + far[:half] * entering
    return pick(is_last, entering, other[half:] + other[:half] * entering)[:, None]


def rows_for(axis, place, stack):
    bit = lax.axis_index(axis)
    low, high = (lax.index_in_dim(stack, i, place, keepdims=False) for i in (0, 1))
    return pick(bit, low, high), pick(bit, high, low)


def token_grad_kernel(offset, *refs):
    pieces, (near, away, out, left, right) = refs[:8], refs[8:]
    rows = pieces[0].shape[0]

    @pl.when(pl.program_id(0) == 0)
    def _():
        for i in range(8):
            held = (near if i < 4 else away)[i % 4]
            left[:, i * rows : (i + 1) * rows] = held[:, offset : offset + rows]

    fill(right, [p[...] for p in pieces])
    out[...] = dot(left[...], right[...]).astype(BF16)


def token_grad(near, away, second, pieces):
    rows, width = pieces[0].shape
    held = near.shape[1]
    tile = 640
    piece = pl.BlockSpec((rows, tile), lambda j: (0, j))
    whole = pl.BlockSpec(near.shape, lambda j: (0, 0, 0), pipeline_mode=pl.Buffered(1))
    return pl.pallas_call(
        partial(token_grad_kernel, second * rows),
        grid=(width // tile,),
        in_specs=[piece] * 8 + [whole, whole],
        out_specs=pl.BlockSpec((held, tile), lambda j: (0, j)),
        out_shape=jax.ShapeDtypeStruct((held, width), BF16),
        scratch_shapes=[pltpu.VMEM((held, 8 * rows), BF16), pltpu.VMEM((8 * rows, tile), BF16)],
        compiler_params=params(),
        cost_estimate=cost(16 * held * rows * width, 20 * rows * width),
        name="token_grad",
    )(*pieces, near, away)


def total_of_all(value, line):
    far = lax.axis_size(SZ)
    held = value.reshape(far, 2, 2, 2, -1)
    for place, axis in ((3, WC), (2, WX), (1, SY)):
        mine, send = rows_for(axis, place, held)
        got = swap(line.mark(send), axis)
        yield
        mine, got = line(mine, got)
        held = mine + got
    here = lax.axis_index(SZ)
    mine = lax.dynamic_index_in_dim(held, here, 0, keepdims=False)
    blocks = [
        lax.dynamic_index_in_dim(held, (here - steps) % far, 0, keepdims=False)
        for steps in range(1, far)
    ]
    line.mark(mine)
    blocks = [around(block, steps) for steps, block in enumerate(blocks, 1)]
    yield
    yield sum(line(*blocks), mine)


def scatter_far(value):
    return lax.psum_scatter(value, SZ, scatter_dimension=0, tiled=True)


def local(
    inputs,
    positions,
    cotangent,
    gain,
    w_x,
    w_y,
    conv_w,
    conv_b,
    gate_a,
    bias_a,
    gate_i,
    bias_i,
    decay_log,
    w_out,
    gain2,
    w_gate,
    w_up,
    w_down,
):
    batches, length, features = inputs.shape
    rows = batches * length
    head = gate_a.shape[1]
    taps = conv_w.shape[0]
    held = w_gate.shape[1]
    far = lax.axis_size(SZ)
    wx, wc, sy = (lax.axis_index(a) for a in (WX, WC, SY))
    as_row = lambda v: v.reshape(1, features)
    cube = lambda v: v.reshape(batches, length, features)
    flat = lambda v: v.reshape(rows, features)

    line = Line()
    sz = lax.axis_index(SZ)
    parity = sz % 2
    spots = jnp.stack([sz, parity, sy]).astype(jnp.int32)
    edge = length - (taps - 1)
    places = positions[..., None]
    half = 2 * rows
    low = lambda v: v.astype(BF16)
    wide = lambda v: v.astype(F32)
    plain = (features // far) % 128 != 0 or far > 4
    pull_of, share_of, grad_of = (
        (share_pull_plain, share_plain, unit_grad_plain) if plain else (share_pull, share, unit_grad)
    )

    joined_rows = lambda own, other: jnp.concatenate([own, other], axis=0)
    core = lambda value: swap(value, WC)
    oth_x, oth_y, oth_out = core(w_x), core(w_y), core(w_out)
    own_gates = jnp.concatenate([gate_a, gate_i], axis=1)
    gates = lax.all_gather(own_gates, (WX, WC), axis=0, tiled=True)
    cot = flat(cotangent)
    cot_all = lax.all_gather(cot, SZ)
    source = wide(flat(inputs))
    norm_scale = lax.rsqrt(jnp.mean(source * source, axis=-1, keepdims=True) + 1e-06)
    normed = low(source * norm_scale * gain)
    keep, send = split_columns(normed, wx, wc)
    line.mark(send)
    recv = swap(send, WX)
    normed_turned = line.mark(line(normed)[0].T)

    line.hold(oth_y, oth_out)
    recv, keep, this, other = line(recv, keep, w_x, oth_x)
    sent, own_x = project(recv, keep, joined_rows(this, other))
    line.mark(sent)
    recv_x = swap(sent, WX)
    recv, keep, this, other = line(recv, keep, w_y, oth_y)
    sent, own_y = project(recv, keep, joined_rows(this, other))
    line.mark(sent)
    sent = line.mark(joined_rows(*line(sent, cot)))
    w_out = line.mark(joined_rows(*line(w_out, oth_out)))
    received = swap(after(sent, recv_x), WX)
    own_x, recv_x, own_y = cube(own_x), cube(recv_x), cube(own_y)
    tail_own, tail_recv = line(own_x[:, edge:], recv_x[:, edge:])
    tail = along_seq(line.mark(low(tail_own + wide(tail_recv))), 1)
    own_x, recv_x, tail, gates = line(own_x, recv_x, tail, gates)
    halo = jnp.pad(wide(tail), ((0, 0), (HALO - (taps - 1), 0), (0, 0)))
    branch_x, conv, gate_rec, gate_in, running, local_state, ends = recur(
        own_x,
        recv_x,
        halo,
        places,
        conv_w,
        as_row(conv_b),
        gates,
        as_row(bias_a),
        as_row(bias_i),
        as_row(decay_log),
    )
    line.mark(ends)
    other_ends = swap(ends, SY)
    ends, other_ends = line(ends, other_ends)
    joined = line.mark(carry_join(ends, other_ends, sy, 1))
    arrived = carry_shifts(joined, 1)
    own_y, received = line(own_y, received)
    recv_y, cot_x = cube(received[:rows]), received[rows:]
    branch_y = line.mark(gelu_pair(own_y + wide(recv_y))[0])
    carry = carry_finish(*tied_carry(line, other_ends, arrived), sy, 1)
    mixed = flat(low((local_state + running * carry) * branch_y))
    keep, send = split_columns(mixed, wx, wc)
    line.mark(send)
    recv = swap(send, WX)
    cot_core, cot_both = core(cot), core(cot_x)
    both_turned = line.mark(jnp.concatenate([normed_turned, line(mixed)[0].T], axis=1))
    line.hold(cot_core, cot_both)
    sent, own = project(*line(recv, keep, w_out))
    line.mark(sent)
    recv = swap(sent, WX)
    pulled_units = line.mark(pull_units(line(cot, cot_x, cot_core, cot_both), w_down))
    own, recv = line(own, recv)
    stream = source + own + wide(recv)
    second_scale = lax.rsqrt(jnp.mean(stream * stream, axis=-1, keepdims=True) + 1e-06)
    normed_two = line.mark(low(stream * second_scale * gain2))

    normed_x, normed_core = swap(normed_two, WX), core(normed_two)
    turned = both_turned.reshape(far, 2, 2, 2, features // (8 * far), half)
    cot_others = line.mark(jnp.roll(*line(cot_all), -sz, axis=0)[1:])
    normed_x, cot_others = line(normed_x, cot_others)
    cot_x_far = swap(cot_others, WX)
    normed_both = core(normed_x)
    pair = line.mark(joined_rows(*line(normed_two, normed_x)))
    normed_here = (lax.all_gather(pair, SZ),)
    mine_x, send_x = rows_for(WX, 2, *line(turned))
    got_x = swap(line.mark(send_x), WX)
    hidden, gate_grad, up_grad = acted = units(
        line(normed_two, normed_x, normed_core, normed_both), w_gate, w_up, pulled_units
    )
    line.mark(hidden)
    mine_y, send_y = rows_for(SY, 2, jnp.stack(line(mine_x, got_x)))
    got_y = swap(line.mark(send_y), SY)
    pulled = units_back(*line(gate_grad, up_grad), w_gate, w_up)
    line.mark(pulled[0])
    pulled_both, pulled_core = core(pulled[3]), core(pulled[2])
    line.hold(pulled_core)
    pulled_there, pulled_both = line(pulled[1], pulled_both)
    for_x = line.mark(low(wide(pulled_there) + wide(pulled_both)))
    from_x = swap(for_x, WX)
    cot_core_all = core(cot_all)
    made = units_made(*line(hidden), w_down)
    line.mark(made[0])
    line.hold(cot_core_all)
    mine_y, got_y = line(mine_y, got_y)
    near, send = rows_for(WC, 2, jnp.concatenate([mine_y, got_y], axis=0))
    near, send = (v.reshape(4, features // 8, half) for v in (near, send))
    away = core(line.mark(send))
    cot_x, cot_x_far = line(cot_x, cot_x_far)
    cot_x_all = line.mark(jnp.concatenate([cot_x[None], cot_x_far], axis=0))
    cot_here, cot_there = (cot_all, cot_x_all), (cot_core_all, core(cot_x_all))
    line.hold(away, cot_there[1])
    pulled_here, pulled_core, from_x = line(pulled[0], pulled_core, from_x)
    grad_normed_two = wide(pulled_here) + wide(pulled_core) + wide(from_x)
    weighted_two = grad_normed_two * gain2
    grad_stream = (
        wide(cot)
        + weighted_two * second_scale
        - stream * second_scale**3 * jnp.mean(weighted_two * stream, axis=-1, keepdims=True)
    )
    grad_gain2 = jnp.sum(grad_normed_two * stream * second_scale, axis=0)
    grad_proj = line.mark(low(grad_stream))
    proj_x, proj_y = swap(grad_proj, WX), swap(grad_proj, SY)
    proj_core = core(grad_proj)
    pull_here = line.mark(pull_of(spots, line(*cot_here), w_down))

    def shared(gathered, pulled):
        *gathered, pulled = line(*gathered, pulled)
        acts = share_of(spots, gathered, w_gate, w_up, pulled)
        line.mark(acts[0])
        return acts

    def unit_sums(here, there, kinds):
        acts = [line(acted[k], acts_here[k], acts_there[k]) for k in kinds]
        outs = grad_of(spots, line(*here), line(*there), acts)
        line.mark(outs[0])
        return [(outs[2 * i], swap(outs[2 * i + 1], SY)) for i in range(len(kinds))]

    def unit_join(mine, got):
        mine, got = line(mine, got)
        both = low(mine + wide(got))
        own, other = pick(parity, both[0], both[1]), pick(parity, both[1], both[0])
        line.mark(other)
        return own, partner_far(other)

    window, offset = window_of(held)

    def unit_final(own, other):
        own, other = line(own, other)
        parts = pick(parity, own, other), pick(parity, other, own)
        return wide(jnp.concatenate([parts[0], parts[1][:, window - offset :]], axis=1))

    def token_sums(second, *pieces):
        grad = token_grad(*line(near, away), second, line(*pieces))
        return scatter_far(line.mark(grad))

    line.hold(proj_y, proj_core, *normed_here)
    proj_x, grad_proj = line(proj_x, grad_proj)
    sent, own = project_back([(proj_x, grad_proj, w_out)])
    line.mark(sent)
    sent, proj_xy = swap(sent, WX), swap(proj_x, SY)
    proj_x_core, proj_y_core = core(proj_x), core(proj_y)
    pull_there = line.mark(pull_of(spots, line(*cot_there), w_down))
    line.hold(proj_xy, proj_x_core, proj_y_core)
    sent, own = line(sent, own)
    grad_mixed = cube(join_columns(own, wide(sent), wx, wc))
    line.mark(grad_mixed)
    grad_pre, behind, local_grad, back_ends = unroll(
        *line(grad_mixed, own_y, recv_y, running, local_state, carry, gate_rec),
        places,
        as_row(decay_log),
        head,
    )
    line.mark(back_ends)
    grad_pre = flat(grad_pre)
    other_ends = swap(back_ends, SY)
    pre_x, pre_y = swap(grad_pre, WX), swap(grad_pre, SY)
    proj_xy_core, pre_core = core(proj_xy), core(grad_pre)
    line.hold(proj_xy_core, pre_core)
    back_ends, other_ends = line(back_ends, other_ends)
    joined = line.mark(carry_join(back_ends, other_ends, sy, -1))
    arrived = carry_shifts(joined, -1)
    acts_here = shared(normed_here, pull_here)
    other_ends, arrived, pre_x, pre_y = line_tree(line, other_ends, arrived, pre_x, pre_y)
    carry_back = carry_finish(other_ends, arrived, sy, -1)
    line.mark(carry_back)
    pre_xy, pre_x_core, pre_y_core = swap(pre_y, WX), core(pre_x), core(pre_y)
    normed_there = (core(after(normed_here[0], carry_back)),)
    spread, earlier, grad_wa, grad_wi, sums = recur_back(
        *line(behind, local_grad, carry_back, running, local_state, carry),
        gate_rec,
        gate_in,
        conv,
        branch_x,
        halo,
        places,
        conv_w,
        gates,
        as_row(decay_log),
    )
    line.mark(earlier)
    later = along_seq(low(earlier[:, HALO - (taps - 1) :]), -1)
    out_sums = token_sums(
        1, grad_proj, proj_x, proj_y, proj_xy, proj_core, proj_x_core, proj_y_core, proj_xy_core
    )
    line.hold(pre_x_core, pre_y_core, pre_xy)
    spread, later = line(spread, later)
    grad_branch = flat(low(spread + jnp.pad(wide(later), ((0, 0), (edge, 0), (0, 0)))))
    line.mark(grad_branch)
    grad_x, grad_y = swap(grad_branch, WX), swap(grad_branch, SY)
    grad_core = core(grad_branch)
    grad_wa, grad_wi, sums, grad_gain2 = line(grad_wa, grad_wi, sums, grad_gain2)
    small = jnp.concatenate([grad_gain2[None], sums], axis=0)
    small = low(jnp.pad(small.T, ((0, 0), (0, 128 - small.shape[0]))))
    rest = jnp.concatenate([grad_wa, grad_wi, small], axis=1)
    rest = line.mark(rest).reshape(far, 2, 2, 2, features // (8 * far), -1)

    def rest_step(axis, place, value):
        mine, send = rows_for(axis, place, value)
        line.mark(send)
        return mine, swap(send, axis)

    def rest_join(mine, got):
        mine, got = line(mine, got)
        return low(wide(mine) + wide(got))

    rest = rest_step(WC, 3, *line(rest))
    line.hold(grad_core, rest[1])
    acts_there = shared(normed_there, pull_there)
    grad_x, grad_branch, grad_y, pre_xy = line(grad_x, grad_branch, grad_y, pre_xy)
    grad_xy, grad_x_core, grad_y_core = swap(grad_y, WX), core(grad_x), core(grad_y)
    pre_xy_core = core(pre_xy)
    rest = rest_step(WX, 2, rest_join(*rest))
    sent, own = project_back(
        [
            (grad_x, grad_branch, joined_rows(w_x, oth_x)),
            (*line(pre_x, grad_pre), joined_rows(w_y, oth_y)),
        ]
    )
    line.mark(sent)
    line.hold(grad_x_core, grad_y_core, pre_xy_core, grad_xy)
    sent = swap(sent, WX)
    rest = rest_step(SY, 1, rest_join(*rest))
    (down,) = unit_sums(cot_here, cot_there, [0])
    y_sums = token_sums(
        0, grad_pre, pre_x, pre_y, pre_xy, pre_core, pre_x_core, pre_y_core, pre_xy_core
    )
    line.hold(out_sums)
    rest = scatter_far(line.mark(rest_join(*rest).reshape(features // 8, -1)))
    grad_xy_core = core(after(grad_xy, down[0]))
    line.hold(grad_xy_core)
    (gate,) = unit_sums(normed_here, normed_there, [1])
    x_sums = token_sums(
        0, grad_branch, grad_x, grad_y, grad_xy, grad_core, grad_x_core, grad_y_core, grad_xy_core
    )
    line.hold(sent)
    down = unit_join(*down)
    (up,) = unit_sums(normed_here, normed_there, [2])
    gate = unit_join(*gate)
    made_both, made_core = core(made[3]), core(made[2])
    line.hold(made_both, made_core)
    sent, own = line(sent, own)
    grad_normed = join_columns(own, wide(sent), wx, wc)
    weighted = grad_normed * gain
    input_grad = (
        grad_stream
        + weighted * norm_scale
        - source * norm_scale**3 * jnp.mean(weighted * source, axis=-1, keepdims=True)
    )
    grad_gain = jnp.sum(grad_normed * source * norm_scale, axis=0)
    grad_gain, input_grad = tie(grad_gain, input_grad)
    line.mark(grad_gain)
    gain_total = total_of_all(grad_gain, line)
    next(gain_total)
    made_there, made_both = line(made[1], made_both)
    made_x = swap(line.mark(low(wide(made_there) + wide(made_both))), WX)
    up = unit_join(*up)
    next(gain_total)
    down_grad = line.mark(unit_final(*down).T)
    next(gain_total)
    made_here, made_core, made_x = line(made[0], made_core, made_x)
    output = line.mark(low(stream + wide(made_here) + wide(made_core) + wide(made_x)))
    next(gain_total)
    gate_grad = line.mark(unit_final(*gate))
    up_grad = line.mark(unit_final(*up))
    grad_gain = line.mark(next(gain_total))
    out_sums, y_sums, rest, x_sums = (
        line.mark(wide(*line(v))) for v in (out_sums, y_sums, rest, x_sums)
    )
    grads = rest[:, 2 * head :]
    return (
        cube(output),
        cube(input_grad),
        grad_gain,
        x_sums,
        y_sums,
        grads[:, 1 : 1 + taps].T,
        grads[:, 1 + taps],
        rest[:, :head],
        grads[:, 2 + taps],
        rest[:, head : 2 * head],
        grads[:, 3 + taps],
        grads[:, 4 + taps],
        out_sums,
        grads[:, 0],
        gate_grad,
        up_grad,
        down_grad,
    )


def solution(mesh):
    seq, wt = mesh.devices.shape
    split = Mesh(mesh.devices.reshape(seq // 2, 2, wt // 2, 2), (SZ, SY, WX, WC))
    s, w = (SZ, SY), (WX, WC)
    everywhere = (SZ, SY, WX, WC)
    return jax.shard_map(
        local,
        mesh=split,
        in_specs=(
            P(w, s, None),
            P(w, s),
            P(w, s, None),
            P(),
            P(w, None),
            P(w, None),
            P(),
            P(),
            P(w, None),
            P(),
            P(w, None),
            P(),
            P(),
            P(w, None),
            P(),
            P(None, w),
            P(None, w),
            P(w, None),
        ),
        out_specs=(
            P(w, s, None),
            P(w, s, None),
            P(everywhere),
            P(everywhere, None),
            P(everywhere, None),
            P(None, everywhere),
            P(everywhere),
            P(everywhere, None),
            P(everywhere),
            P(everywhere, None),
            P(everywhere),
            P(everywhere),
            P(everywhere, None),
            P(everywhere),
            P(s, w),
            P(s, w),
            P(w, s),
        ),
        check_vma=False,
    )
```

```python
from functools import partial

import jax
import jax.numpy as jnp
from jax import lax
from jax.experimental import pallas as pl
from jax.experimental.pallas import tpu as pltpu
from jax.sharding import Mesh
from jax.sharding import PartitionSpec as P

SZ, SY, WX, WC = ("sz", "sy", "wx", "wc")
F32, BF16 = (jnp.float32, jnp.bfloat16)
HALO = 8
ROOT_2_PI = 0.7978845608028654
CUBIC = 0.044715
VMEM_GRANT = 58 << 20
COST_SHARE = 0.02
HEADS_EACH = 2


def swap(value, axis):
    return lax.ppermute(value, axis, [(0, 1), (1, 0)])


def shift(value, axis, steps):
    count = lax.axis_size(axis)
    initial, last = (max(0, -steps), min(count, count - steps))
    return lax.ppermute(value, axis, [(source, source + steps) for source in range(initial, last)])


def around(value, steps):
    count = lax.axis_size(SZ)
    return lax.ppermute(value, SZ, [((to + steps) % count, to) for to in range(count)])


def partner_far(value):
    count = lax.axis_size(SZ)
    return lax.ppermute(value, SZ, [(source, source ^ 1) for source in range(count)])


def along_seq(value, steps):
    count = lax.axis_size(SZ) * lax.axis_size(SY)
    initial, last = (max(0, -steps), min(count, count - steps))
    return lax.ppermute(
        value, (SZ, SY), [(source, source + steps) for source in range(initial, last)]
    )


def pick(bit, zero, one):
    return jnp.where(bit == 0, zero, one)


def after(value, *others):
    return lax.optimization_barrier((value, *others))[0]


def tie(*values):
    return lax.optimization_barrier(values)


class Line:
    def __init__(self):
        self.last = None
        self.held = []

    def __call__(self, *values):
        others = self.held + ([] if self.last is None else [self.last])
        self.held = []
        return lax.optimization_barrier((*values, *others))[: len(values)]

    def hold(self, *values):
        self.held += values

    def mark(self, value):
        self.last = value
        return value


def gelu_pair(value):
    square = value * value
    tanh = jnp.tanh(ROOT_2_PI * value * (1.0 + CUBIC * square))
    half = 0.5 * (1.0 + tanh)
    slope = half + 0.5 * value * (1.0 - tanh * tanh) * (
        ROOT_2_PI * (1.0 + 3.0 * CUBIC * square)
    )
    return value * half, slope


def dot(left, right):
    return jnp.dot(left, right, preferred_element_type=F32)


def dot_nt(left, right):
    return lax.dot_general(left, right, (((1,), (1,)), ((), ())), preferred_element_type=F32)


def dot_tn(left, right):
    return lax.dot_general(left, right, (((0,), (0,)), ((), ())), preferred_element_type=F32)


def params():
    return pltpu.CompilerParams(
        dimension_semantics=("arbitrary",), vmem_limit_bytes=VMEM_GRANT
    )


def cost(flops, nbytes):
    return pl.CostEstimate(
        flops=int(flops * COST_SHARE), bytes_accessed=int(nbytes * COST_SHARE), transcendentals=0
    )


def split_columns(value, wx, wc):
    quarter = value.shape[-1] // 4
    parts = [value[..., i * quarter : (i + 1) * quarter] for i in range(4)]
    near = [pick(wx, parts[0], parts[2]), pick(wx, parts[1], parts[3])]
    far = [pick(wx, parts[2], parts[0]), pick(wx, parts[3], parts[1])]
    keep = jnp.concatenate([pick(wc, near[0], near[1]), pick(wc, near[1], near[0])], axis=-1)
    send = jnp.concatenate([pick(wc, far[0], far[1]), pick(wc, far[1], far[0])], axis=-1)
    return keep, send


def join_columns(near, far, wx, wc):
    near = [pick(wc, near[0], near[1]), pick(wc, near[1], near[0])]
    far = [pick(wc, far[0], far[1]), pick(wc, far[1], far[0])]
    return jnp.concatenate(
        [
            pick(wx, near[0], far[0]),
            pick(wx, near[1], far[1]),
            pick(wx, far[0], near[0]),
            pick(wx, far[1], near[1]),
        ],
        axis=-1,
    )


def project(recv, keep, weight):
    rows = recv.shape[0]
    total = dot(jnp.concatenate([recv, keep], axis=0), weight)
    return total[:rows].astype(BF16), total[rows:]


def project_back(terms):
    rows = terms[0][0].shape[0]
    total = 0.0
    for recv, own, weight in terms:
        total = total + dot_nt(jnp.concatenate([recv, own], axis=0), weight)
    half = total.shape[1] // 2
    total = jnp.stack([total[:, :half], total[:, half:]])
    return total[:, :rows].astype(BF16), total[:, rows:]


def less_one_exp(value):
    series = 1.0
    for n in (9, 8, 7, 6, 5, 4, 3, 2):
        series = 1.0 + value * (1.0 / n) * series
    return jnp.where(value > -0.5, -value * series, 1.0 - jnp.exp(value))


def shifted_down(value, steps, fill):
    edge = jnp.full((value.shape[0], steps, value.shape[2]), fill, F32)
    return jnp.concatenate([edge, value[:, : value.shape[1] - steps]], axis=1)


def shifted_up(value, steps, fill):
    edge = jnp.full((value.shape[0], steps, value.shape[2]), fill, F32)
    return jnp.concatenate([value[:, steps:], edge], axis=1)


def scan_rows(decay, driven, mover):
    steps = 1
    while steps < decay.shape[1]:
        driven = driven + decay * mover(driven, steps, 0.0)
        decay = decay * mover(decay, steps, 1.0)
        steps *= 2
    return decay, driven


def tap_mask(places, offset):
    return (places >= offset).astype(F32)


def by_head(flat, gate, product):
    head = gate.shape[1]
    spans = [slice(i, i + head) for i in range(0, flat.shape[1], head)]
    return jnp.concatenate([product(flat[:, s], gate[s]) for s in spans], axis=1)


def recur_kernel(
    own,
    recv,
    halo,
    places,
    conv_w,
    conv_b,
    gate_a,
    gate_i,
    bias_a,
    bias_i,
    decay_log,
    branch_out,
    conv_out,
    rec_out,
    in_out,
    run_out,
    state_out,
    ends_out,
):
    batches, length, width = own.shape
    branch = (own[...] + recv[...].astype(F32)).astype(BF16)
    branch_out[...] = branch
    extended = jnp.concatenate([halo[...], branch.astype(F32)], axis=1)
    spot = places[...]
    total = jnp.zeros((batches, length, width), F32) + conv_b[...][None]
    for offset in range(conv_w.shape[0]):
        moved = extended[:, HALO - offset : HALO - offset + length]
        total = total + conv_w[offset : offset + 1][None] * moved * tap_mask(spot, offset)
    conv = total.astype(BF16)
    conv_out[...] = conv
    flat = conv.reshape(batches * length, width)
    shape = (batches, length, width)
    gate_rec = jax.nn.sigmoid(by_head(flat, gate_a, dot) + bias_a[...]).reshape(shape)
    gate_in = jax.nn.sigmoid(by_head(flat, gate_i, dot) + bias_i[...]).reshape(shape)
    rec_out[...] = gate_rec
    in_out[...] = gate_in
    log_a = -8.0 * gate_rec * jnp.exp(decay_log[...])[None]
    alive = tap_mask(spot, 1)
    root = jnp.sqrt(less_one_exp(2.0 * log_a))
    multiplier = alive * root + (1.0 - alive)
    decay = jnp.exp(log_a) * alive
    driven = conv.astype(F32) * gate_in * multiplier
    running, state = scan_rows(decay, driven, shifted_down)
    run_out[...] = running
    state_out[...] = state
    for b in range(batches):
        ends_out[b : b + 1] = running[b, length - 1 :]
        ends_out[batches + b : batches + b + 1] = state[b, length - 1 :]


def head_specs(batches, length, head, taps, group=1):
    head = head * group
    tokens = pl.BlockSpec((batches, length, head), lambda h: (0, 0, h))
    edge = pl.BlockSpec((batches, HALO, head), lambda h: (0, 0, h))
    place = pl.BlockSpec((batches, length, 1), lambda h: (0, 0, 0))
    row = pl.BlockSpec((1, head), lambda h: (0, h))
    tap = pl.BlockSpec((taps, head), lambda h: (0, h))
    gates = [
        pl.BlockSpec((head, head // group), lambda h: (h, 0)),
        pl.BlockSpec((head, head // group), lambda h: (h, 1)),
    ]
    ends = pl.BlockSpec((2 * batches, head), lambda h: (0, h))
    carry = pl.BlockSpec((batches, 1, head), lambda h: (0, 0, h))
    return tokens, edge, place, row, tap, gates, ends, carry


def recur(own, recv, halo, places, conv_w, conv_b, gates, bias_a, bias_i, decay_log):
    batches, length, features = own.shape
    head = gates.shape[1] // 2
    tokens, edge, place, row, tap, gate, ends, _ = head_specs(
        batches, length, head, conv_w.shape[0], HEADS_EACH
    )
    full = lambda dtype: jax.ShapeDtypeStruct((batches, length, features), dtype)
    return pl.pallas_call(
        recur_kernel,
        grid=(features // (head * HEADS_EACH),),
        in_specs=[tokens, tokens, edge, place, tap, row, *gate, row, row, row],
        out_specs=[tokens] * 6 + [ends],
        out_shape=[full(BF16), full(BF16)]
        + [full(F32)] * 4
        + [jax.ShapeDtypeStruct((2 * batches, features), F32)],
        compiler_params=params(),
        cost_estimate=cost(200 * batches * length * features, 40 * batches * length * features),
        name="recur",
    )(own, recv, halo, places, conv_w, conv_b, gates, gates, bias_a, bias_i, decay_log)


def unroll_kernel(
    mixed_grad,
    own_y,
    recv_y,
    running,
    local_state,
    carry,
    gate_rec,
    places,
    decay_log,
    pre_out,
    behind_out,
    local_out,
    ends_out,
):
    batches, length, _ = mixed_grad.shape
    pulled = mixed_grad[...].astype(F32)
    branch_y, slope = gelu_pair(own_y[...] + recv_y[...].astype(F32))
    state = local_state[...] + running[...] * carry[...]
    pre_out[...] = (pulled * state * slope).astype(BF16)
    log_a = -8.0 * gate_rec[...] * jnp.exp(decay_log[...])[None]
    decay = jnp.exp(log_a) * tap_mask(places[...], 1)
    following = shifted_up(decay, 1, 1.0)
    behind, local = scan_rows(following, pulled * branch_y, shifted_up)
    behind_out[...] = behind
    local_out[...] = local
    for b in range(batches):
        ends_out[b : b + 1] = running[b, length - 1 :, :]
        ends_out[batches + b : batches + b + 1] = decay[b, :1] * local[b, :1]


def unroll(mixed_grad, own_y, recv_y, running, local_state, carry, gate_rec, places, decay_log, head):
    batches, length, features = mixed_grad.shape
    tokens, _, place, row, _, _, ends, carried = head_specs(batches, length, head, 1, HEADS_EACH)
    full = lambda dtype: jax.ShapeDtypeStruct((batches, length, features), dtype)
    return pl.pallas_call(
        unroll_kernel,
        grid=(features // (head * HEADS_EACH),),
        in_specs=[tokens] * 5 + [carried, tokens, place, row],
        out_specs=[tokens] * 3 + [ends],
        out_shape=[full(BF16), full(F32), full(F32)]
        + [jax.ShapeDtypeStruct((2 * batches, features), F32)],
        compiler_params=params(),
        cost_estimate=cost(200 * batches * length * features, 40 * batches * length * features),
        name="unroll",
    )(mixed_grad, own_y, recv_y, running, local_state, carry, gate_rec, places, decay_log)


def recur_back_kernel(
    behind,
    local_grad,
    carry_back,
    running,
    local_state,
    carry,
    gate_rec,
    gate_in,
    conv,
    branch,
    halo,
    places,
    conv_w,
    gate_a,
    gate_i,
    decay_log,
    spread_out,
    earlier_out,
    wa_out,
    wi_out,
    sums_out,
):
    batches, length, width = behind.shape
    shape = (batches, length, width)
    rows = batches * length
    spot = places[...]
    alive = tap_mask(spot, 1)
    rate = jnp.exp(decay_log[...])[None]
    rec, inner = gate_rec[...], gate_in[...]
    log_a = -8.0 * rec * rate
    raw = jnp.exp(log_a)
    root = jnp.sqrt(less_one_exp(2.0 * log_a))
    multiplier = alive * root + (1.0 - alive)
    conv_low = conv[...]
    conv_full = conv_low.astype(F32)
    grad_state = local_grad[...] + behind[...] * carry_back[...]
    state = local_state[...] + running[...] * carry[...]
    before = jnp.concatenate([carry[...], state[:, : length - 1]], axis=1)
    scaled = grad_state * conv_full * inner
    grad_log = alive * raw * (grad_state * before - scaled * raw / root)
    grad_a = grad_log * (-8.0 * rate) * rec * (1.0 - rec)
    grad_i = scaled * multiplier * (1.0 - inner)
    low_a = grad_a.astype(BF16).reshape(rows, width)
    low_i = grad_i.astype(BF16).reshape(rows, width)
    pulled = grad_state * inner * multiplier
    pulled = pulled + (
        by_head(low_a, gate_a, dot_nt) + by_head(low_i, gate_i, dot_nt)
    ).reshape(shape)
    pulled = pulled.astype(BF16).astype(F32)
    flat = conv_low.reshape(rows, width)
    head = gate_a.shape[1]
    for i in range(0, width, head):
        span = slice(i, i + head)
        wa_out[span] = dot_tn(flat[:, span], low_a[:, span]).astype(BF16)
        wi_out[span] = dot_tn(flat[:, span], low_i[:, span]).astype(BF16)
    extended = jnp.concatenate([halo[...], branch[...].astype(F32)], axis=1)
    taps = conv_w.shape[0]
    spread = jnp.zeros((batches, length + HALO, width), F32)
    blank = jnp.zeros((batches, HALO, width), F32)
    sums = []
    add = lambda value: jnp.sum(value.reshape(rows, width), axis=0, keepdims=True)
    for offset in range(taps):
        masked = pulled * tap_mask(spot, offset)
        weighted = jnp.concatenate([blank, conv_w[offset : offset + 1][None] * masked], axis=1)
        spread = spread + (shifted_up(weighted, offset, 0.0) if offset else weighted)
        sums.append(add(masked * extended[:, HALO - offset : HALO - offset + length]))
    earlier_out[...] = spread[:, :HALO]
    spread_out[...] = spread[:, HALO:]
    sums += [add(pulled), add(grad_a), add(grad_i), add(grad_log * log_a)]
    sums_out[...] = jnp.concatenate(sums, axis=0)


def recur_back(
    behind,
    local_grad,
    carry_back,
    running,
    local_state,
    carry,
    gate_rec,
    gate_in,
    conv,
    branch,
    halo,
    places,
    conv_w,
    gates,
    decay_log,
):
    batches, length, features = behind.shape
    head = gates.shape[1] // 2
    taps = conv_w.shape[0]
    tokens, edge, place, row, tap, gate, _, carried = head_specs(
        batches, length, head, taps, HEADS_EACH
    )
    block = pl.BlockSpec((head * HEADS_EACH, head), lambda h: (h, 0))
    return pl.pallas_call(
        recur_back_kernel,
        grid=(features // (head * HEADS_EACH),),
        in_specs=[tokens, tokens, carried, tokens, tokens, carried]
        + [tokens] * 4
        + [edge, place, tap, *gate, row],
        out_specs=[
            tokens,
            edge,
            block,
            block,
            pl.BlockSpec((taps + 4, head * HEADS_EACH), lambda h: (0, h)),
        ],
        out_shape=[
            jax.ShapeDtypeStruct((batches, length, features), F32),
            jax.ShapeDtypeStruct((batches, HALO, features), F32),
            jax.ShapeDtypeStruct((features, head), BF16),
            jax.ShapeDtypeStruct((features, head), BF16),
            jax.ShapeDtypeStruct((taps + 4, features), F32),
        ],
        compiler_params=params(),
        cost_estimate=cost(300 * batches * length * features, 50 * batches * length * features),
        name="recur_back",
    )(
        behind,
        local_grad,
        carry_back,
        running,
        local_state,
        carry,
        gate_rec,
        gate_in,
        conv,
        branch,
        halo,
        places,
        conv_w,
        gates,
        gates,
        decay_log,
    )


def unit_step(gate_pre, up_pre, pulled, hidden_out, gate_out, up_out):
    act, slope = gelu_pair(gate_pre)
    hidden_out[...] = (act * up_pre).astype(BF16)
    gate_out[...] = (pulled * up_pre * slope).astype(BF16)
    up_out[...] = (pulled * act).astype(BF16)


def fill(target, pieces):
    start = 0
    for piece in pieces:
        target[start : start + piece.shape[0]] = piece
        start += piece.shape[0]


def units_kernel(count, *refs):
    pieces, (w_gate, w_up, pulled, hidden_out, gate_out, up_out, tokens) = refs[:count], refs[count:]

    @pl.when(pl.program_id(0) == 0)
    def _():
        fill(tokens, [p[...] for p in pieces])

    gate_pre, up_pre = dot(tokens[...], w_gate[...]), dot(tokens[...], w_up[...])
    unit_step(gate_pre, up_pre, pulled[...].astype(F32), hidden_out, gate_out, up_out)


def units(pieces, w_gate, w_up, pulled):
    count = len(pieces)
    rows, width = pieces[0].shape
    held = w_gate.shape[1]
    tile = 640
    whole = pl.BlockSpec((rows, width), lambda j: (0, 0), pipeline_mode=pl.Buffered(1))
    column = pl.BlockSpec((width, tile), lambda j: (0, j))
    out = pl.BlockSpec((count * rows, tile), lambda j: (0, j))
    return pl.pallas_call(
        partial(units_kernel, count),
        grid=(held // tile,),
        in_specs=[whole] * count + [column, column, out],
        out_specs=[out] * 3,
        out_shape=[jax.ShapeDtypeStruct((count * rows, held), BF16)] * 3,
        scratch_shapes=[pltpu.VMEM((count * rows, width), BF16)],
        compiler_params=params(),
        cost_estimate=cost(4 * count * rows * width * held, 4 * width * held),
        name="units",
    )(*pieces, w_gate, w_up, pulled)


def pull_units_kernel(count, *refs):
    pieces, (w_down, out, tokens) = refs[:count], refs[count:]

    @pl.when(pl.program_id(0) == 0)
    def _():
        fill(tokens, [p[...] for p in pieces])

    out[...] = dot_nt(tokens[...], w_down[...]).astype(BF16)


def pull_units(pieces, w_down):
    count = len(pieces)
    rows, width = pieces[0].shape
    held = w_down.shape[0]
    tile = 640
    whole = pl.BlockSpec((rows, width), lambda j: (0, 0), pipeline_mode=pl.Buffered(1))
    return pl.pallas_call(
        partial(pull_units_kernel, count),
        grid=(held // tile,),
        in_specs=[whole] * count + [pl.BlockSpec((tile, width), lambda j: (j, 0))],
        out_specs=pl.BlockSpec((count * rows, tile), lambda j: (0, j)),
        out_shape=jax.ShapeDtypeStruct((count * rows, held), BF16),
        scratch_shapes=[pltpu.VMEM((count * rows, width), BF16)],
        compiler_params=params(),
        cost_estimate=cost(2 * count * rows * width * held, 2 * width * held),
        name="pull_units",
    )(*pieces, w_down)


def spill(total, outs):
    rows = outs[0].shape[0]
    for i, out in enumerate(outs):
        out[...] = total[i * rows : (i + 1) * rows].astype(BF16)


def units_back_kernel(gate, up, w_gate, w_up, *outs):
    spill(dot_nt(gate[...], w_gate[...]) + dot_nt(up[...], w_up[...]), outs)


def units_back(gate, up, w_gate, w_up):
    tile = 640
    rows = gate.shape[0]
    width, held = w_gate.shape
    whole = pl.BlockSpec((rows, held), lambda j: (0, 0), pipeline_mode=pl.Buffered(1))
    row = pl.BlockSpec((tile, held), lambda j: (j, 0))
    return pl.pallas_call(
        units_back_kernel,
        grid=(width // tile,),
        in_specs=[whole, whole, row, row],
        out_specs=[pl.BlockSpec((rows // 4, tile), lambda j: (0, j))] * 4,
        out_shape=[jax.ShapeDtypeStruct((rows // 4, width), BF16)] * 4,
        compiler_params=params(),
        cost_estimate=cost(4 * rows * width * held, 4 * width * held),
        name="units_back",
    )(gate, up, w_gate, w_up)


def units_made_kernel(hidden, w_down, *outs):
    spill(dot(hidden[...], w_down[...]), outs)


def units_made(hidden, w_down):
    tile = 1280
    rows, held = hidden.shape
    width = w_down.shape[1]
    return pl.pallas_call(
        units_made_kernel,
        grid=(width // tile,),
        in_specs=[
            pl.BlockSpec((rows, held), lambda j: (0, 0), pipeline_mode=pl.Buffered(1)),
            pl.BlockSpec((held, tile), lambda j: (0, j)),
        ],
        out_specs=[pl.BlockSpec((rows // 4, tile), lambda j: (0, j))] * 4,
        out_shape=[jax.ShapeDtypeStruct((rows // 4, width), BF16)] * 4,
        compiler_params=params(),
        cost_estimate=cost(2 * rows * width * held, 2 * width * held),
        name="units_made",
    )(hidden, w_down)


def window_of(held):
    width = -(-held // 2 // 128) * 128
    return width, held - width


def at_distance(places, gathered, steps):
    count = gathered[0].shape[0]
    return [part[(places[0] + steps) % count] for part in gathered]


def others(places, gathered):
    count = gathered[0].shape[0]
    return [v for steps in range(1, count) for v in at_distance(places, gathered, steps)]


def share_pull_kernel(count, places, *refs):
    gathered, (w_down, out, tokens) = refs[:count], refs[count:]

    @pl.when(pl.program_id(0) == 0)
    def _():
        fill(tokens, others(places, gathered))

    out[...] = dot_nt(tokens[...], w_down[...]).astype(BF16)


def share_kernel(count, places, *refs):
    gathered, refs = refs[:count], refs[count:]
    w_gate, w_up, pulled, hidden_out, gate_out, up_out, tokens = refs

    @pl.when(pl.program_id(0) == 0)
    def _():
        fill(tokens, others(places, gathered))

    gate_pre, up_pre = dot(tokens[...], w_gate[...]), dot(tokens[...], w_up[...])
    unit_step(gate_pre, up_pre, pulled[...].astype(F32), hidden_out, gate_out, up_out)


def share_call(kernel, places, gathered, weights, more, outs, name):
    count, rows, width = gathered[0].shape
    tile = 512
    held = weights[0].shape[0] if weights[0].shape[1] == width else weights[0].shape[1]
    window, offset = window_of(held)
    total = len(gathered) * (count - 1) * rows
    specs = []
    for weight in weights:
        if weight.shape[1] == width:
            specs.append(
                pl.BlockSpec(
                    (pl.Element(tile), pl.Element(width)),
                    lambda j, places: (pl.multiple_of(places[1] * offset + j * tile, 128), 0),
                )
            )
        else:
            specs.append(
                pl.BlockSpec(
                    (pl.Element(width), pl.Element(tile)),
                    lambda j, places: (0, pl.multiple_of(places[1] * offset + j * tile, 128)),
                )
            )
    out = pl.BlockSpec((total, tile), lambda j, places: (0, j))
    whole = pl.BlockSpec(
        gathered[0].shape, lambda j, places: (0, 0, 0), pipeline_mode=pl.Buffered(1)
    )
    return pl.pallas_call(
        partial(kernel, len(gathered)),
        grid_spec=pltpu.PrefetchScalarGridSpec(
            num_scalar_prefetch=1,
            grid=(window // tile,),
            in_specs=[whole] * len(gathered) + specs + [out] * len(more),
            out_specs=[out] * outs,
            scratch_shapes=[pltpu.VMEM((total, width), BF16)],
        ),
        out_shape=[jax.ShapeDtypeStruct((total, window), BF16)] * outs,
        compiler_params=params(),
        cost_estimate=cost(
            2 * len(weights) * total * width * window, 2 * len(weights) * width * window
        ),
        name=name,
    )(places, *gathered, *weights, *more)


def share_pull(places, gathered, w_down):
    return share_call(share_pull_kernel, places, gathered, [w_down], [], 1, "share_pull")[0]


def share(places, gathered, w_gate, w_up, pulled):
    return share_call(share_kernel, places, gathered, [w_gate, w_up], [pulled], 3, "share")


def unit_grad_kernel(count, kinds, places, *refs):
    here, there, refs = refs[:count], refs[count : 2 * count], refs[2 * count :]
    acts, outs = refs[: 3 * kinds], refs[3 * kinds : 5 * kinds]
    left, whole = refs[5 * kinds :]
    block = whole.shape[0] // 2
    fill(
        left,
        at_distance(places, here, 0)
        + at_distance(places, there, 0)
        + others(places, here)
        + others(places, there),
    )
    own = pl.multiple_of(places[2] * block, block)
    other = pl.multiple_of((1 - places[2]) * block, block)
    for kind in range(kinds):
        parts = acts[3 * kind : 3 * kind + 3]
        total, start = None, 0
        for part in parts:
            size = part.shape[0]
            term = dot_tn(left[start : start + size], part[...])
            total = term if total is None else total + term
            start += size
        whole[...] = total
        outs[2 * kind][0] = whole[pl.ds(own, block)]
        outs[2 * kind + 1][0] = whole[pl.ds(other, block)].astype(BF16)


def unit_grad(places, here, there, acts):
    kinds = len(acts)
    count, rows, features = here[0].shape
    window, offset = window_of(acts[0][0].shape[1])
    width = features // count
    total = 2 * len(here) * count * rows
    once = pl.Buffered(1)
    gathered = pl.BlockSpec((count, rows, width), lambda i, p: (0, 0, 2 * (p[0] // 2) + i))
    mine = pl.BlockSpec(
        (pl.Element(2 * len(here) * rows), pl.Element(window)),
        lambda i, p: (0, pl.multiple_of(p[1] * offset, 128)),
        pipeline_mode=once,
    )
    act = pl.BlockSpec(acts[0][1].shape, lambda i, p: (0, 0), pipeline_mode=once)
    out = pl.BlockSpec((1, width // 2, window), lambda i, p: (i, 0, 0))
    shape = (2, width // 2, window)
    return pl.pallas_call(
        partial(unit_grad_kernel, len(here), kinds),
        grid_spec=pltpu.PrefetchScalarGridSpec(
            num_scalar_prefetch=1,
            grid=(2,),
            in_specs=[gathered] * (2 * len(here)) + [mine, act, act] * kinds,
            out_specs=[out] * (2 * kinds),
            scratch_shapes=[
                pltpu.VMEM((total, width), BF16),
                pltpu.VMEM((width, window), F32),
            ],
        ),
        out_shape=[jax.ShapeDtypeStruct(shape, d) for d in (F32, BF16)] * kinds,
        compiler_params=params(),
        cost_estimate=cost(4 * kinds * total * width * window, 2 * kinds * total * window),
        name="unit_grad",
    )(places, *here, *there, *[a for v in acts for a in v])


def window_part(value, places, axis):
    window, offset = window_of(value.shape[axis])
    return lax.dynamic_slice_in_dim(value, places[1] * offset, window, axis=axis)


def others_plain(places, gathered):
    features = gathered[0].shape[2]
    rolled = [jnp.roll(v, -places[0], axis=0)[1:] for v in gathered]
    return jnp.concatenate(rolled, axis=1).reshape(-1, features)


def share_pull_plain(places, gathered, w_down):
    tokens = others_plain(places, gathered)
    return dot_nt(tokens, window_part(w_down, places, 0)).astype(BF16)


def share_plain(places, gathered, w_gate, w_up, pulled):
    tokens = others_plain(places, gathered)
    act, slope = gelu_pair(dot(tokens, window_part(w_gate, places, 1)))
    up_pre = dot(tokens, window_part(w_up, places, 1))
    pulled = pulled.astype(F32)
    return [v.astype(BF16) for v in (act * up_pre, pulled * up_pre * slope, pulled * act)]


def unit_grad_plain(places, here, there, acts):
    count, _, features = here[0].shape
    block = features // (2 * count)
    at = lambda v: lax.dynamic_index_in_dim(v, places[0], 0, keepdims=False)
    own = [at(v) for v in (*here, *there)]
    tokens = jnp.concatenate(
        own + [others_plain(places, here), others_plain(places, there)], axis=0
    )
    tokens = lax.dynamic_slice_in_dim(tokens, places[0] // 2 * 4 * block, 4 * block, axis=1)
    outs = []
    for own, *rest in acts:
        right = jnp.concatenate([window_part(own, places, 1), *rest], axis=0)
        whole = dot_tn(tokens, right).reshape(2, 2, block, -1)
        outs.append(pick(places[2], whole[:, 0], whole[:, 1]))
        outs.append(pick(places[2], whole[:, 1], whole[:, 0]).astype(BF16))
    return outs


def carry_join(ends, other, bit, direction):
    half = ends.shape[0] // 2
    is_last = bit if direction > 0 else 1 - bit
    first_end = pick(is_last, ends[half:], other[half:])
    last_end = pick(is_last, other[half:], ends[half:])
    last_run = pick(is_last, other[:half], ends[:half])
    return jnp.concatenate(
        [ends[:half] * other[:half], last_run * first_end + last_end], axis=0
    )


def carry_shifts(joined, direction):
    return [shift(joined, SZ, direction * k) for k in range(1, lax.axis_size(SZ))]


def line_tree(line, *values):
    leaves, tree = jax.tree.flatten(values)
    arrays = iter(line(*[v for v in leaves if not isinstance(v, int)]))
    return jax.tree.unflatten(tree, [v if isinstance(v, int) else next(arrays) for v in leaves])


def tied_carry(line, other, arrived):
    other, *arrived = line(other, *arrived)
    return other, arrived


def carry_finish(other, arrived, bit, direction):
    half = other.shape[0] // 2
    is_last = bit if direction > 0 else 1 - bit
    entering = jnp.zeros_like(other[half:])
    for far in reversed(arrived):
        entering = far[half:] + far[:half] * entering
    return pick(is_last, entering, other[half:] + other[:half] * entering)[:, None]


def rows_for(axis, place, stack):
    bit = lax.axis_index(axis)
    low, high = (lax.index_in_dim(stack, i, place, keepdims=False) for i in (0, 1))
    return pick(bit, low, high), pick(bit, high, low)


def token_grad_kernel(offset, *refs):
    pieces, (near, away, out, left, right) = refs[:8], refs[8:]
    rows = pieces[0].shape[0]

    @pl.when(pl.program_id(0) == 0)
    def _():
        for i in range(8):
            held = (near if i < 4 else away)[i % 4]
            left[:, i * rows : (i + 1) * rows] = held[:, offset : offset + rows]

    fill(right, [p[...] for p in pieces])
    out[...] = dot(left[...], right[...]).astype(BF16)


def token_grad(near, away, second, pieces):
    rows, width = pieces[0].shape
    held = near.shape[1]
    tile = 640
    piece = pl.BlockSpec((rows, tile), lambda j: (0, j))
    whole = pl.BlockSpec(near.shape, lambda j: (0, 0, 0), pipeline_mode=pl.Buffered(1))
    return pl.pallas_call(
        partial(token_grad_kernel, second * rows),
        grid=(width // tile,),
        in_specs=[piece] * 8 + [whole, whole],
        out_specs=pl.BlockSpec((held, tile), lambda j: (0, j)),
        out_shape=jax.ShapeDtypeStruct((held, width), BF16),
        scratch_shapes=[pltpu.VMEM((held, 8 * rows), BF16), pltpu.VMEM((8 * rows, tile), BF16)],
        compiler_params=params(),
        cost_estimate=cost(16 * held * rows * width, 20 * rows * width),
        name="token_grad",
    )(*pieces, near, away)


def total_of_all(value, line):
    far = lax.axis_size(SZ)
    held = value.reshape(far, 2, 2, 2, -1)
    for place, axis in ((3, WC), (2, WX), (1, SY)):
        mine, send = rows_for(axis, place, held)
        got = swap(line.mark(send), axis)
        yield
        mine, got = line(mine, got)
        held = mine + got
    here = lax.axis_index(SZ)
    mine = lax.dynamic_index_in_dim(held, here, 0, keepdims=False)
    blocks = [
        lax.dynamic_index_in_dim(held, (here - steps) % far, 0, keepdims=False)
        for steps in range(1, far)
    ]
    line.mark(mine)
    blocks = [around(block, steps) for steps, block in enumerate(blocks, 1)]
    yield
    yield sum(line(*blocks), mine)


def scatter_far(value):
    return lax.psum_scatter(value, SZ, scatter_dimension=0, tiled=True)


def local(
    inputs,
    positions,
    cotangent,
    gain,
    w_x,
    w_y,
    conv_w,
    conv_b,
    gate_a,
    bias_a,
    gate_i,
    bias_i,
    decay_log,
    w_out,
    gain2,
    w_gate,
    w_up,
    w_down,
):
    batches, length, features = inputs.shape
    rows = batches * length
    head = gate_a.shape[1]
    taps = conv_w.shape[0]
    held = w_gate.shape[1]
    far = lax.axis_size(SZ)
    wx, wc, sy = (lax.axis_index(a) for a in (WX, WC, SY))
    as_row = lambda v: v.reshape(1, features)
    cube = lambda v: v.reshape(batches, length, features)
    flat = lambda v: v.reshape(rows, features)

    line = Line()
    sz = lax.axis_index(SZ)
    parity = sz % 2
    spots = jnp.stack([sz, parity, sy]).astype(jnp.int32)
    edge = length - (taps - 1)
    places = positions[..., None]
    half = 2 * rows
    low = lambda v: v.astype(BF16)
    wide = lambda v: v.astype(F32)
    plain = (features // far) % 128 != 0 or far > 4
    pull_of, share_of, grad_of = (
        (share_pull_plain, share_plain, unit_grad_plain) if plain else (share_pull, share, unit_grad)
    )

    joined_rows = lambda own, other: jnp.concatenate([own, other], axis=0)
    core = lambda value: swap(value, WC)
    oth_x, oth_y, oth_out = core(w_x), core(w_y), core(w_out)
    own_gates = jnp.concatenate([gate_a, gate_i], axis=1)
    gates = lax.all_gather(own_gates, (WX, WC), axis=0, tiled=True)
    cot = flat(cotangent)
    cot_all = lax.all_gather(cot, SZ)
    source = wide(flat(inputs))
    norm_scale = lax.rsqrt(jnp.mean(source * source, axis=-1, keepdims=True) + 1e-06)
    normed = low(source * norm_scale * gain)
    keep, send = split_columns(normed, wx, wc)
    line.mark(send)
    recv = swap(send, WX)
    normed_turned = line.mark(line(normed)[0].T)

    line.hold(oth_y, oth_out)
    recv, keep, this, other = line(recv, keep, w_x, oth_x)
    sent, own_x = project(recv, keep, joined_rows(this, other))
    line.mark(sent)
    recv_x = swap(sent, WX)
    recv, keep, this, other = line(recv, keep, w_y, oth_y)
    sent, own_y = project(recv, keep, joined_rows(this, other))
    line.mark(sent)
    sent = line.mark(joined_rows(*line(sent, cot)))
    w_out = line.mark(joined_rows(*line(w_out, oth_out)))
    received = swap(after(sent, recv_x), WX)
    own_x, recv_x, own_y = cube(own_x), cube(recv_x), cube(own_y)
    tail_own, tail_recv = line(own_x[:, edge:], recv_x[:, edge:])
    tail = along_seq(line.mark(low(tail_own + wide(tail_recv))), 1)
    own_x, recv_x, tail, gates = line(own_x, recv_x, tail, gates)
    halo = jnp.pad(wide(tail), ((0, 0), (HALO - (taps - 1), 0), (0, 0)))
    branch_x, conv, gate_rec, gate_in, running, local_state, ends = recur(
        own_x,
        recv_x,
        halo,
        places,
        conv_w,
        as_row(conv_b),
        gates,
        as_row(bias_a),
        as_row(bias_i),
        as_row(decay_log),
    )
    line.mark(ends)
    other_ends = swap(ends, SY)
    ends, other_ends = line(ends, other_ends)
    joined = line.mark(carry_join(ends, other_ends, sy, 1))
    arrived = carry_shifts(joined, 1)
    own_y, received = line(own_y, received)
    recv_y, cot_x = cube(received[:rows]), received[rows:]
    branch_y = line.mark(gelu_pair(own_y + wide(recv_y))[0])
    line.hold(cot_all)
    carry = carry_finish(*tied_carry(line, other_ends, arrived), sy, 1)
    mixed = flat(low((local_state + running * carry) * branch_y))
    keep, send = split_columns(mixed, wx, wc)
    line.mark(send)
    recv = swap(send, WX)
    cot_core, cot_both = core(cot), core(cot_x)
    cot_x_all = lax.all_gather(cot_x, SZ)
    both_turned = line.mark(jnp.concatenate([normed_turned, line(mixed)[0].T], axis=1))
    line.hold(cot_core, cot_both)
    sent, own = project(*line(recv, keep, w_out))
    line.mark(sent)
    recv = swap(sent, WX)
    pulled_units = line.mark(pull_units(line(cot, cot_x, cot_core, cot_both), w_down))
    own, recv = line(own, recv)
    stream = source + own + wide(recv)
    second_scale = lax.rsqrt(jnp.mean(stream * stream, axis=-1, keepdims=True) + 1e-06)
    normed_two = line.mark(low(stream * second_scale * gain2))

    normed_x, normed_core = swap(normed_two, WX), core(normed_two)
    turned = both_turned.reshape(far, 2, 2, 2, features // (8 * far), half)
    line.hold(cot_x_all)
    (normed_x,) = line(normed_x)
    normed_both = core(normed_x)
    pair = line.mark(joined_rows(*line(normed_two, normed_x)))
    normed_here = (lax.all_gather(pair, SZ),)
    mine_x, send_x = rows_for(WX, 2, *line(turned))
    got_x = swap(line.mark(send_x), WX)
    hidden, gate_grad, up_grad = acted = units(
        line(normed_two, normed_x, normed_core, normed_both), w_gate, w_up, pulled_units
    )
    line.mark(hidden)
    mine_y, send_y = rows_for(SY, 2, jnp.stack(line(mine_x, got_x)))
    got_y = swap(line.mark(send_y), SY)
    pulled = units_back(*line(gate_grad, up_grad), w_gate, w_up)
    line.mark(pulled[0])
    pulled_both, pulled_core = core(pulled[3]), core(pulled[2])
    line.hold(pulled_core)
    pulled_there, pulled_both = line(pulled[1], pulled_both)
    for_x = line.mark(low(wide(pulled_there) + wide(pulled_both)))
    from_x = swap(for_x, WX)
    made = units_made(*line(hidden), w_down)
    line.mark(made[0])
    mine_y, got_y = line(mine_y, got_y)
    near, send = rows_for(WC, 2, jnp.concatenate([mine_y, got_y], axis=0))
    near, send = (v.reshape(4, features // 8, half) for v in (near, send))
    away = core(line.mark(send))
    line.hold(away)
    pulled_here, pulled_core, from_x, cot_x_all = line(pulled[0], pulled_core, from_x, cot_x_all)
    cot_here = (cot_all, cot_x_all)
    grad_normed_two = wide(pulled_here) + wide(pulled_core) + wide(from_x)
    weighted_two = grad_normed_two * gain2
    grad_stream = (
        wide(cot)
        + weighted_two * second_scale
        - stream * second_scale**3 * jnp.mean(weighted_two * stream, axis=-1, keepdims=True)
    )
    grad_gain2 = jnp.sum(grad_normed_two * stream * second_scale, axis=0)
    grad_proj = line.mark(low(grad_stream))
    proj_x, proj_y = swap(grad_proj, WX), swap(grad_proj, SY)
    proj_core = core(grad_proj)
    cot_here = line(*cot_here)
    cot_there = tuple(core(v) for v in cot_here)
    pull_here = line.mark(pull_of(spots, cot_here, w_down))

    def shared(gathered, pulled):
        *gathered, pulled = line(*gathered, pulled)
        acts = share_of(spots, gathered, w_gate, w_up, pulled)
        line.mark(acts[0])
        return acts

    def unit_sums(here, there, kinds):
        acts = [line(acted[k], acts_here[k], acts_there[k]) for k in kinds]
        outs = grad_of(spots, line(*here), line(*there), acts)
        line.mark(outs[0])
        return [(outs[2 * i], swap(outs[2 * i + 1], SY)) for i in range(len(kinds))]

    def unit_join(mine, got):
        mine, got = line(mine, got)
        both = low(mine + wide(got))
        own, other = pick(parity, both[0], both[1]), pick(parity, both[1], both[0])
        line.mark(other)
        return own, partner_far(other)

    window, offset = window_of(held)

    def unit_final(own, other):
        own, other = line(own, other)
        parts = pick(parity, own, other), pick(parity, other, own)
        return wide(jnp.concatenate([parts[0], parts[1][:, window - offset :]], axis=1))

    def token_sums(second, *pieces):
        grad = token_grad(*line(near, away), second, line(*pieces))
        return scatter_far(line.mark(grad))

    line.hold(proj_y, proj_core, *cot_there)
    proj_x, grad_proj = line(proj_x, grad_proj)
    sent, own = project_back([(proj_x, grad_proj, w_out)])
    line.mark(sent)
    sent, proj_xy = swap(sent, WX), swap(proj_x, SY)
    proj_x_core, proj_y_core = core(proj_x), core(proj_y)
    pull_there = line.mark(pull_of(spots, line(*cot_there), w_down))
    line.hold(proj_xy, proj_x_core, proj_y_core, *normed_here)
    sent, own = line(sent, own)
    grad_mixed = cube(join_columns(own, wide(sent), wx, wc))
    line.mark(grad_mixed)
    grad_pre, behind, local_grad, back_ends = unroll(
        *line(grad_mixed, own_y, recv_y, running, local_state, carry, gate_rec),
        places,
        as_row(decay_log),
        head,
    )
    line.mark(back_ends)
    grad_pre = flat(grad_pre)
    other_ends = swap(back_ends, SY)
    pre_x, pre_y = swap(grad_pre, WX), swap(grad_pre, SY)
    proj_xy_core, pre_core = core(proj_xy), core(grad_pre)
    line.hold(proj_xy_core, pre_core)
    back_ends, other_ends = line(back_ends, other_ends)
    joined = line.mark(carry_join(back_ends, other_ends, sy, -1))
    arrived = carry_shifts(joined, -1)
    acts_here = shared(normed_here, pull_here)
    other_ends, arrived, pre_x, pre_y = line_tree(line, other_ends, arrived, pre_x, pre_y)
    carry_back = carry_finish(other_ends, arrived, sy, -1)
    line.mark(carry_back)
    pre_xy, pre_x_core, pre_y_core = swap(pre_y, WX), core(pre_x), core(pre_y)
    normed_there = (core(after(normed_here[0], carry_back)),)
    spread, earlier, grad_wa, grad_wi, sums = recur_back(
        *line(behind, local_grad, carry_back, running, local_state, carry),
        gate_rec,
        gate_in,
        conv,
        branch_x,
        halo,
        places,
        conv_w,
        gates,
        as_row(decay_log),
    )
    line.mark(earlier)
    later = along_seq(low(earlier[:, HALO - (taps - 1) :]), -1)
    out_sums = token_sums(
        1, grad_proj, proj_x, proj_y, proj_xy, proj_core, proj_x_core, proj_y_core, proj_xy_core
    )
    line.hold(pre_x_core, pre_y_core, pre_xy)
    spread, later = line(spread, later)
    grad_branch = flat(low(spread + jnp.pad(wide(later), ((0, 0), (edge, 0), (0, 0)))))
    line.mark(grad_branch)
    grad_x, grad_y = swap(grad_branch, WX), swap(grad_branch, SY)
    grad_core = core(grad_branch)
    grad_wa, grad_wi, sums, grad_gain2 = line(grad_wa, grad_wi, sums, grad_gain2)
    small = jnp.concatenate([grad_gain2[None], sums], axis=0)
    small = low(jnp.pad(small.T, ((0, 0), (0, 128 - small.shape[0]))))
    rest = jnp.concatenate([grad_wa, grad_wi, small], axis=1)
    rest = line.mark(rest).reshape(far, 2, 2, 2, features // (8 * far), -1)

    def rest_step(axis, place, value):
        mine, send = rows_for(axis, place, value)
        line.mark(send)
        return mine, swap(send, axis)

    def rest_join(mine, got):
        mine, got = line(mine, got)
        return low(wide(mine) + wide(got))

    rest = rest_step(WC, 3, *line(rest))
    line.hold(grad_core, rest[1])
    acts_there = shared(normed_there, pull_there)
    grad_x, grad_branch, grad_y, pre_xy = line(grad_x, grad_branch, grad_y, pre_xy)
    grad_xy, grad_x_core, grad_y_core = swap(grad_y, WX), core(grad_x), core(grad_y)
    pre_xy_core = core(pre_xy)
    rest = rest_step(WX, 2, rest_join(*rest))
    sent, own = project_back(
        [
            (grad_x, grad_branch, joined_rows(w_x, oth_x)),
            (*line(pre_x, grad_pre), joined_rows(w_y, oth_y)),
        ]
    )
    line.mark(sent)
    line.hold(grad_x_core, grad_y_core, pre_xy_core, grad_xy)
    sent = swap(sent, WX)
    (down,) = unit_sums(cot_here, cot_there, [0])
    rest = rest_step(SY, 1, rest_join(*rest))
    y_sums = token_sums(
        0, grad_pre, pre_x, pre_y, pre_xy, pre_core, pre_x_core, pre_y_core, pre_xy_core
    )
    line.hold(out_sums)
    rest = scatter_far(line.mark(rest_join(*rest).reshape(features // 8, -1)))
    grad_xy_core = core(after(grad_xy, down[0]))
    line.hold(grad_xy_core)
    (gate,) = unit_sums(normed_here, normed_there, [1])
    x_sums = token_sums(
        0, grad_branch, grad_x, grad_y, grad_xy, grad_core, grad_x_core, grad_y_core, grad_xy_core
    )
    line.hold(sent)
    down = unit_join(*down)
    (up,) = unit_sums(normed_here, normed_there, [2])
    gate = unit_join(*gate)
    made_both, made_core = core(made[3]), core(made[2])
    line.hold(made_both, made_core)
    sent, own = line(sent, own)
    grad_normed = join_columns(own, wide(sent), wx, wc)
    weighted = grad_normed * gain
    input_grad = (
        grad_stream
        + weighted * norm_scale
        - source * norm_scale**3 * jnp.mean(weighted * source, axis=-1, keepdims=True)
    )
    grad_gain = jnp.sum(grad_normed * source * norm_scale, axis=0)
    grad_gain, input_grad = tie(grad_gain, input_grad)
    line.mark(grad_gain)
    gain_total = total_of_all(grad_gain, line)
    next(gain_total)
    made_there, made_both = line(made[1], made_both)
    made_x = swap(line.mark(low(wide(made_there) + wide(made_both))), WX)
    up = unit_join(*up)
    next(gain_total)
    down_grad = line.mark(unit_final(*down).T)
    next(gain_total)
    made_here, made_core, made_x = line(made[0], made_core, made_x)
    output = line.mark(low(stream + wide(made_here) + wide(made_core) + wide(made_x)))
    next(gain_total)
    gate_grad = line.mark(unit_final(*gate))
    up_grad = line.mark(unit_final(*up))
    grad_gain = line.mark(next(gain_total))
    out_sums, y_sums, rest, x_sums = (
        line.mark(wide(*line(v))) for v in (out_sums, y_sums, rest, x_sums)
    )
    grads = rest[:, 2 * head :]
    return (
        cube(output),
        cube(input_grad),
        grad_gain,
        x_sums,
        y_sums,
        grads[:, 1 : 1 + taps].T,
        grads[:, 1 + taps],
        rest[:, :head],
        grads[:, 2 + taps],
        rest[:, head : 2 * head],
        grads[:, 3 + taps],
        grads[:, 4 + taps],
        out_sums,
        grads[:, 0],
        gate_grad,
        up_grad,
        down_grad,
    )


def solution(mesh):
    seq, wt = mesh.devices.shape
    split = Mesh(mesh.devices.reshape(seq // 2, 2, wt // 2, 2), (SZ, SY, WX, WC))
    s, w = (SZ, SY), (WX, WC)
    everywhere = (SZ, SY, WX, WC)
    return jax.shard_map(
        local,
        mesh=split,
        in_specs=(
            P(w, s, None),
            P(w, s),
            P(w, s, None),
            P(),
            P(w, None),
            P(w, None),
            P(),
            P(),
            P(w, None),
            P(),
            P(w, None),
            P(),
            P(),
            P(w, None),
            P(),
            P(None, w),
            P(None, w),
            P(w, None),
        ),
        out_specs=(
            P(w, s, None),
            P(w, s, None),
            P(everywhere),
            P(everywhere, None),
            P(everywhere, None),
            P(None, everywhere),
            P(everywhere),
            P(everywhere, None),
            P(everywhere),
            P(everywhere, None),
            P(everywhere),
            P(everywhere),
            P(everywhere, None),
            P(everywhere),
            P(s, w),
            P(s, w),
            P(w, s),
        ),
        check_vma=False,
    )
```
